128 devices in a mesh: ctx: 8 (over z, y_lo), head: 4 (over x), dp: 4 (over y_hi, core).
Axes of the slice: x: 4, y: 4 (y_hi: 2, y_lo: 2; y = y_hi * 2 + y_lo), z: 4, core: 2. Of those that a mesh axis runs over, the one named last changes fastest.
Arguments:
- patch_rows: bfloat16 [24576, 3072], P(('dp', 'ctx'), 'head'), parts along dimension 0, may hold values from -40 to 40
- query_weight: bfloat16 [3072, 3072], P(None, 'head'), may hold values from -0.109375 to 0.109375
- key_weight: bfloat16 [3072, 3072], P(None, 'head'), may hold values from -0.109375 to 0.109375
- value_weight: bfloat16 [3072, 3072], P(None, 'head'), may hold values from -0.109375 to 0.109375
- output_weight: bfloat16 [3072, 3072], P('head'), may hold values from -0.109375 to 0.109375
- tile_slot: int32 [192], P('dp'), parts along dimension 0, may hold values from 0 to 47, as said below
- tile_mask: int32 [192, 48], P('dp'), parts along dimension 0, may hold values from 0 to 1, as said below
Outputs:
- layer_output: bfloat16 [24576, 3072], P(('dp', 'ctx'), 'head'), parts along dimension 0
The draws below stay inside these ranges and needn't reach their ends.
There are 4 independent parts, one for each index of `dp`. The reference program is written for one: setup_inputs(seed, part) draws one part's arguments, and reference() takes and returns one part's arrays. A program takes and returns all parts, laid end to end along the dimension named above; an argument that names none is the same for every part. Nothing has to cross between parts.
Inputs may be any that keep to these rules, and one draw needn't show every extreme that they name: A permutation: loader tile t (rows t*128 to (t+1)*128 - 1 of patch_rows, on loader shard t // 6) becomes context tile tile_slot[t]; context shard c holds context tiles c*6 to (c+1)*6 - 1. The tiles of one loader shard are spread as evenly over the context shards as they can be, so that every loader shard sends exactly 1 tiles to some context shard and none sends more. `tile_mask`: 1 only where both tiles lie in one clip, a run of consecutive context tiles; every tile is live for itself; one clip covers half of the tiles or more.
All inputs are finite; a program needn't handle non-finite values.
Results may differ from the reference program's by a relative error of at most 0.015.
The reference program's roundings to bfloat16 on the way count: a program that leaves them out, or rounds other values in their place, can miss the bound.
Values may be sent and summed in bfloat16 or wider, within the bound.
A program may use at most 128 MiB of HBM per device.

```python
import math
import jax
import jax.numpy as jnp
from jax import lax

D = 3072
HEADS = 24
HDIM = 128
TILE = 128
TILES_DEV = 6
NTILES = 48
TOKENS = 6144


def draw_patch_rows(key, part):
    rows_key = jax.random.fold_in(key, 0)
    values = jax.random.normal(rows_key, (TOKENS, D), jnp.float32)
    return jnp.clip(values, -40.0, 40.0).astype(jnp.bfloat16)


def draw_tile_slot(key, part):
    groups = NTILES // TILES_DEV
    shuffle_key, start_key, order_key = jax.random.split(key, 3)
    shuffle = jax.random.permutation(shuffle_key, groups).astype(jnp.int32)
    offsets = jax.random.permutation(start_key, groups).astype(jnp.int32)
    source = jnp.arange(groups, dtype=jnp.int32)[:, None]
    column = jnp.arange(TILES_DEV, dtype=jnp.int32)[None, :]
    dest = shuffle[(offsets[source] + column) % groups]
    scores = jax.random.randint(order_key, (groups, TILES_DEV), 0, 1 << 20) * TILES_DEV + jnp.arange(TILES_DEV, dtype=jnp.int32)[None, :]
    order = jnp.argsort(scores, axis=1).astype(jnp.int32)
    local = order[dest, column + 0 * dest]
    slot = dest * TILES_DEV + local
    return slot.reshape(NTILES).astype(jnp.int32)


def draw_tile_mask(key, part):
    size_key, first_key, cut_key, reach_key, thin_key = jax.random.split(key, 5)
    big = jax.random.randint(size_key, (), (NTILES + 1) // 2, NTILES + 1)
    first = jax.random.randint(first_key, (), 0, NTILES - big + 1)
    places = jnp.arange(NTILES, dtype=jnp.int32)
    cuts = jax.random.randint(cut_key, (NTILES,), 0, 3) == 0
    inside = (places > first) & (places < first + big)
    starts = (places == 0) | (places == first) | (places == first + big) | cuts & jnp.logical_not(inside)
    clip = jnp.cumsum(starts.astype(jnp.int32)).astype(jnp.int32)
    reach = jax.random.randint(reach_key, (NTILES + 2,), 2, 5)
    level = reach[clip]
    gap = jnp.abs(places[:, None] - places[None, :])
    powers = 2 ** jnp.arange(16, dtype=jnp.int32)
    octave = jnp.sum((gap[:, :, None] >= powers[None, None, :]).astype(jnp.int32), axis=2) - 1
    step = 2 ** jnp.maximum(octave - level[:, None], 0)
    dropped = jax.random.randint(thin_key, (NTILES, NTILES), 0, 4) == 0
    keep = jnp.logical_not(dropped) | (gap == 0)
    live = (clip[:, None] == clip[None, :]) & (gap % step == 0) & keep
    return live.astype(jnp.int32)


def level_of(stream_key, shape, pieces, smallest, high):
    level = 1.0
    for position, blocks in pieces:
        steps = jax.random.uniform(jax.random.fold_in(jax.random.fold_in(stream_key, 6), position), (blocks,), jnp.float32, smallest / len(pieces), high / len(pieces))
        level = level * jnp.repeat(jnp.exp(steps), shape[position] // blocks).reshape((-1,) + (1,) * (len(shape) - 1 - position))
    return level


def bell_draw(key, extent, deviation, most, shards=(), held_as=jnp.bfloat16):
    level = level_of(key, extent, shards, -0.22, 0.18) if shards else 1.0
    result = jax.random.normal(key, extent, jnp.float32) * deviation * level
    return jnp.minimum(jnp.maximum(result, -most), most).astype(held_as)


def setup_inputs(seed: int = 0, part: int = 0) -> dict:
    key_of = jax.random.split(jax.random.key(seed), 8)
    own_keys = jax.random.split(jax.random.fold_in(key_of[7], part), 8)
    return {
        "patch_rows": draw_patch_rows(jax.random.fold_in(jax.random.fold_in(key_of[7], part), 71), part),
        "query_weight": bell_draw(key_of[1], (D, D), D ** -0.5, 0.109375, ((1, 4),)),
        "key_weight": bell_draw(key_of[2], (D, D), D ** -0.5, 0.109375, ((1, 4),)),
        "value_weight": bell_draw(key_of[3], (D, D), D ** -0.5, 0.109375, ((1, 4),)),
        "output_weight": bell_draw(key_of[4], (D, D), D ** -0.5, 0.109375, ((0, 4),)),
        "tile_slot": draw_tile_slot(jax.random.fold_in(jax.random.fold_in(key_of[7], part), 71), part),
        "tile_mask": draw_tile_mask(jax.random.fold_in(jax.random.fold_in(key_of[7], part), 71), part),
    }


MASKED = -1e+30

def reference(patch_rows, query_weight, key_weight, value_weight, output_weight, tile_slot, tile_mask):
    loader_tiles = patch_rows.reshape(NTILES, TILE, D)
    context_tiles = jnp.zeros_like(loader_tiles).at[tile_slot].set(loader_tiles)
    context_rows = context_tiles.reshape(TOKENS, D)
    query_rows = jnp.dot(context_rows, query_weight, preferred_element_type=jnp.float32).astype(jnp.bfloat16)
    key_rows = jnp.dot(context_rows, key_weight, preferred_element_type=jnp.float32).astype(jnp.bfloat16)
    value_rows = jnp.dot(context_rows, value_weight, preferred_element_type=jnp.float32).astype(jnp.bfloat16)
    live_pairs = jnp.repeat(jnp.repeat(tile_mask == 1, TILE, axis=0), TILE, axis=1)
    score_scale = 1.0 / math.sqrt(HDIM)

    def split_heads(row_block):
        return row_block.reshape(TOKENS, HEADS, HDIM).transpose(1, 0, 2)

    def one_head(inputs):
        query_head, key_head, value_head = inputs
        scores = jnp.dot(query_head, key_head.T, preferred_element_type=jnp.float32) * score_scale
        row_peak = lax.optimization_barrier(jnp.max(jnp.where(live_pairs, scores, MASKED), axis=1, keepdims=True))
        weights = jnp.where(live_pairs, jnp.exp(scores - row_peak), 0.0)
        weight_sum = lax.optimization_barrier(jnp.sum(weights, axis=1, keepdims=True))
        weighted = jnp.dot(weights.astype(jnp.bfloat16), value_head, preferred_element_type=jnp.float32)
        return (weighted / weight_sum).astype(jnp.bfloat16)
    head_outputs = lax.map(one_head, (split_heads(query_rows), split_heads(key_rows), split_heads(value_rows)))
    attended = head_outputs.transpose(1, 0, 2).reshape(TOKENS, D)
    mixed_rows = jnp.dot(attended, output_weight, preferred_element_type=jnp.float32).astype(jnp.bfloat16)
    return mixed_rows.reshape(NTILES, TILE, D)[tile_slot].reshape(TOKENS, D)
```

```python
import math

import jax
import jax.numpy as jnp
from jax import lax
from jax.experimental import pallas as pl
from jax.experimental.pallas import tpu as pltpu
from jax.sharding import PartitionSpec as P

HDIM = 128
TILE = 128
GROUP = 4
LOG2E = 1.4426950408889634


def attend_kernel(
    key_list, value_list, counts, qkv_ref, out_ref, keys_t, values, scores
):
    tiles = qkv_ref.shape[0] // TILE
    pad = key_list.shape[0] // tiles
    factor = LOG2E / math.sqrt(HDIM)

    @pl.when(counts[tiles] == 1)
    def _():
        def prepare(t, carry):
            rows = pl.ds(pl.multiple_of(t * TILE, TILE), TILE)
            keys_t[:, rows] = qkv_ref[rows, HDIM : 2 * HDIM].T
            values[rows, :HDIM] = qkv_ref[rows, 2 * HDIM :]
            values[rows, HDIM:] = jnp.ones((TILE, HDIM), jnp.bfloat16)
            return carry

        lax.fori_loop(0, tiles, prepare, 0)
        values[pl.ds(tiles * TILE, TILE), :] = jnp.zeros((TILE, 2 * HDIM), jnp.bfloat16)

        def query_tile(t, carry):
            rows = pl.ds(pl.multiple_of(t * TILE, TILE), TILE)
            query = qkv_ref[rows, :HDIM]
            steps = (counts[t] + GROUP - 1) // GROUP

            def score_step(g, peak):
                base = t * pad + g * GROUP
                block = jnp.concatenate(
                    [
                        keys_t[:, pl.ds(pl.multiple_of(key_list[base + i] * TILE, TILE), TILE)]
                        for i in range(GROUP)
                    ],
                    axis=1,
                )
                found = jnp.dot(query, block, preferred_element_type=jnp.float32)
                scores[g] = found
                for i in range(GROUP):
                    peak = jnp.maximum(peak, found[:, i * TILE : (i + 1) * TILE])
                return peak

            peak = lax.fori_loop(
                0, steps, score_step, jnp.full((TILE, TILE), -jnp.inf, jnp.float32)
            )
            row_peak = jnp.max(peak, axis=1, keepdims=True) * factor

            def value_step(g, total):
                base = t * pad + g * GROUP
                weight = jnp.exp2(scores[g] * factor - row_peak).astype(jnp.bfloat16)
                block = jnp.concatenate(
                    [
                        values[pl.ds(pl.multiple_of(value_list[base + i] * TILE, TILE), TILE), :]
                        for i in range(GROUP)
                    ],
                    axis=0,
                )
                return total + jnp.dot(weight, block, preferred_element_type=jnp.float32)

            total = lax.fori_loop(
                0, steps, value_step, jnp.zeros((TILE, 2 * HDIM), jnp.float32)
            )
            out_ref[rows, :] = (total[:, :HDIM] / total[:, HDIM:]).astype(jnp.bfloat16)
            return carry

        lax.fori_loop(0, tiles, query_tile, 0)


def attend(key_list, value_list, counts, qkv):
    rows = qkv.shape[0]
    return pl.pallas_call(
        attend_kernel,
        out_shape=jax.ShapeDtypeStruct((rows, HDIM), jnp.bfloat16),
        grid_spec=pltpu.PrefetchScalarGridSpec(
            num_scalar_prefetch=3,
            grid=(1,),
            in_specs=[pl.BlockSpec((rows, 3 * HDIM), lambda i, *_: (0, 0))],
            out_specs=pl.BlockSpec((rows, HDIM), lambda i, *_: (0, 0)),
            scratch_shapes=[
                pltpu.VMEM((HDIM, rows), jnp.bfloat16),
                pltpu.VMEM((rows + TILE, 2 * HDIM), jnp.bfloat16),
                pltpu.VMEM((rows // (TILE * GROUP), TILE, GROUP * TILE), jnp.float32),
            ],
        ),
        compiler_params=pltpu.CompilerParams(vmem_limit_bytes=40 * 1024 * 1024),
        cost_estimate=pl.CostEstimate(
            flops=4 * rows * rows * HDIM, bytes_accessed=8 * rows * HDIM, transcendentals=rows * rows
        ),
        name="attend",
    )(key_list, value_list, counts, qkv)


def live_lists(tile_slot, tile_mask, active):
    tiles = tile_slot.shape[0]
    places = jnp.arange(tiles, dtype=jnp.int32)
    pick = (tile_slot[:, None] == places[None, :]).astype(jnp.float32)
    mask = (tile_mask == 1).astype(jnp.float32)
    live = jnp.dot(jnp.dot(pick, mask), pick.T)
    upper = (places[:, None] <= places[None, :]).astype(jnp.float32)
    rank = jnp.dot(live, upper).astype(jnp.int32) - 1
    counts = rank[:, -1] + 1
    hit = (rank[:, :, None] == places[None, None, :]) & (live[:, :, None] > 0.5)
    listed = jnp.sum(jnp.where(hit, places[None, :, None], 0), axis=1)
    used = places[None, :] < counts[:, None]
    key_list = jnp.where(used, listed, listed[:, :1]).reshape(-1)
    value_list = jnp.where(used, listed, tiles).reshape(-1)
    counts = jnp.concatenate([counts, active.astype(jnp.int32)[None]])
    return key_list, value_list, counts


def project(features, weight):
    return jnp.dot(features, weight, preferred_element_type=jnp.float32).astype(jnp.bfloat16)


def body(patch_rows, query_weight, key_weight, value_weight, output_weight, tile_slot, tile_mask):
    groups = lax.axis_size("ctx")
    shard = lax.axis_index("ctx")
    tokens = patch_rows.shape[0]
    heads = query_weight.shape[1] // HDIM
    slots = [0, 1, 2, 4, 5, 6]
    active = lax.rem(shard, 4) != 3
    key_list, value_list, counts = live_lists(tile_slot, tile_mask, active)
    features = lax.all_gather(patch_rows, "head", axis=1, tiled=True)
    query = project(features, query_weight)
    key = project(features, key_weight)
    value = project(features, value_weight)
    packs = []
    empty = jnp.zeros((tokens, 3 * HDIM), jnp.bfloat16)
    for s in range(groups):
        if s in slots:
            h = slots.index(s)
            cols = slice(h * HDIM, (h + 1) * HDIM)
            packs.append(jnp.concatenate([query[:, cols], key[:, cols], value[:, cols]], axis=1))
        else:
            packs.append(empty)
    sent = lax.all_to_all(jnp.stack(packs), "ctx", split_axis=0, concat_axis=0, tiled=True)
    attended = attend(key_list, value_list, counts, sent.reshape(groups * tokens, 3 * HDIM))
    back = lax.all_to_all(
        attended.reshape(groups, tokens, HDIM), "ctx", split_axis=0, concat_axis=0, tiled=True
    )
    attended = jnp.concatenate([back[s] for s in slots], axis=1)
    partial_out = jnp.dot(attended, output_weight, preferred_element_type=jnp.float32)
    return lax.psum_scatter(
        partial_out.astype(jnp.bfloat16), "head", scatter_dimension=1, tiled=True
    )


def solution(mesh):
    in_specs = (
        P(("dp", "ctx"), "head"),
        P(None, "head"),
        P(None, "head"),
        P(None, "head"),
        P("head", None),
        P("dp"),
        P("dp", None),
    )
    out_specs = P(("dp", "ctx"), "head")
    return jax.shard_map(body, mesh=mesh, in_specs=in_specs, out_specs=out_specs, check_vma=False)
```

```python
import functools
import math

import jax
import jax.numpy as jnp
from jax import lax
from jax.experimental import pallas as pl
from jax.experimental.pallas import tpu as pltpu
from jax.sharding import PartitionSpec as P

HDIM = 128
TILE = 128
GROUP = 8
TOGETHER = 3
FRONT_ROWS = 128
FRONT_AHEAD = 2
MESH = pl.DeviceIdType.MESH
LOG2E = 1.4426950408889634


def attend_kernel(
    order, key_list, value_list, counts, qkv_ref, out_ref, keys_t, values, scores
):
    tiles = qkv_ref.shape[0] // TILE
    pad = key_list.shape[0] // tiles
    stages = tiles // TOGETHER
    factor = LOG2E / math.sqrt(HDIM)

    def at(tile):
        return pl.ds(pl.multiple_of(tile * TILE, TILE), TILE)

    def score_step(queries, stage, g, peaks):
        fresh = []
        for j in range(TOGETHER):
            base = (stage * TOGETHER + j) * pad + g * GROUP
            peak = peaks[j]
            for i in range(0, GROUP, 2):
                block = jnp.concatenate(
                    [keys_t[:, at(key_list[base + i])], keys_t[:, at(key_list[base + i + 1])]], axis=1
                )
                found = jnp.dot(queries[j], block, preferred_element_type=jnp.float32)
                scores[lax.rem(stage, 2), g, j, :, i * TILE : (i + 2) * TILE] = found
                peak = jnp.maximum(peak, jnp.maximum(found[:, :TILE], found[:, TILE:]))
            fresh.append(peak)
        return tuple(fresh)

    def value_step(stage, g, row_peaks, totals):
        fresh = []
        for j in range(TOGETHER):
            base = (stage * TOGETHER + j) * pad + g * GROUP
            weight = jnp.exp2(
                scores[lax.rem(stage, 2), g, j] * factor - row_peaks[j]
            ).astype(jnp.bfloat16)
            block = jnp.concatenate([values[at(value_list[base + i]), :] for i in range(GROUP)], axis=0)
            fresh.append(totals[j] + jnp.dot(weight, block, preferred_element_type=jnp.float32))
        return tuple(fresh)

    def load_queries(stage):
        return [qkv_ref[at(order[stage * TOGETHER + j]), :HDIM] for j in range(TOGETHER)]

    def steps_of(stage):
        return (counts[stage * TOGETHER] + GROUP - 1) // GROUP

    def to_rows(peaks):
        return tuple(
            jnp.broadcast_to(jnp.max(peak, axis=1, keepdims=True) * factor, (TILE, 1)) for peak in peaks
        )

    def finish(stage, totals):
        for j in range(TOGETHER):
            out_ref[at(order[stage * TOGETHER + j]), :] = (
                totals[j][:, :HDIM] / totals[j][:, HDIM:]
            ).astype(jnp.bfloat16)

    low = tuple(jnp.full((TILE, TILE), -jnp.inf, jnp.float32) for _ in range(TOGETHER))
    zero = tuple(jnp.zeros((TILE, 2 * HDIM), jnp.float32) for _ in range(TOGETHER))

    @pl.when(counts[tiles] == 1)
    def _():
        def prepare(t, carry):
            keys_t[:, at(t)] = qkv_ref[at(t), HDIM : 2 * HDIM].T
            values[at(t), :HDIM] = qkv_ref[at(t), 2 * HDIM :]
            values[at(t), HDIM:] = jnp.ones((TILE, HDIM), jnp.bfloat16)
            return carry

        lax.fori_loop(0, tiles, prepare, 0, unroll=2)
        values[pl.ds(tiles * TILE, TILE), :] = jnp.zeros((TILE, 2 * HDIM), jnp.bfloat16)

        queries = load_queries(0)
        peaks = lax.fori_loop(0, steps_of(0), lambda g, p: score_step(queries, 0, g, p), low)

        def stage_body(stage, row_peaks):
            queries = load_queries(stage)

            def both(g, carry):
                peaks, totals = carry
                totals = value_step(stage - 1, g, row_peaks, totals)
                peaks = score_step(queries, stage, g, peaks)
                return peaks, totals

            peaks, totals = lax.fori_loop(0, steps_of(stage - 1), both, (low, zero))
            finish(stage - 1, totals)
            return to_rows(peaks)

        row_peaks = lax.fori_loop(1, stages, stage_body, to_rows(peaks))
        totals = lax.fori_loop(
            0, steps_of(stages - 1), lambda g, t: value_step(stages - 1, g, row_peaks, t), zero
        )
        finish(stages - 1, totals)


def attend(order, key_list, value_list, counts, qkv):
    rows = qkv.shape[0]
    return pl.pallas_call(
        attend_kernel,
        out_shape=jax.ShapeDtypeStruct((rows, HDIM), jnp.bfloat16),
        grid_spec=pltpu.PrefetchScalarGridSpec(
            num_scalar_prefetch=4,
            grid=(1,),
            in_specs=[pl.BlockSpec((rows, 3 * HDIM), lambda i, *_: (0, 0))],
            out_specs=pl.BlockSpec((rows, HDIM), lambda i, *_: (0, 0)),
            scratch_shapes=[
                pltpu.VMEM((HDIM, rows), jnp.bfloat16),
                pltpu.VMEM((rows + TILE, 2 * HDIM), jnp.bfloat16),
                pltpu.VMEM(
                    (2, rows // (TILE * GROUP), TOGETHER, TILE, GROUP * TILE), jnp.float32
                ),
            ],
        ),
        compiler_params=pltpu.CompilerParams(vmem_limit_bytes=52 * 1024 * 1024),
        cost_estimate=pl.CostEstimate(
            flops=4 * rows * rows * HDIM, bytes_accessed=8 * rows * HDIM, transcendentals=rows * rows
        ),
        name="attend",
    )(order, key_list, value_list, counts, qkv)


def live_lists(tile_slot, tile_mask, active):
    tiles = tile_slot.shape[0]
    places = jnp.arange(tiles, dtype=jnp.int32)
    pick = (tile_slot[:, None] == places[None, :]).astype(jnp.float32)
    mask = (tile_mask == 1).astype(jnp.float32)
    size = jnp.sum(mask, axis=1)
    ahead = (size[None, :] > size[:, None]) | (
        (size[None, :] == size[:, None]) & (places[None, :] < places[:, None])
    )
    position = jnp.sum(ahead.astype(jnp.int32), axis=1)
    arrange = (position[None, :] == places[:, None]).astype(jnp.float32)
    chosen = jnp.dot(arrange, pick.T)
    order = jnp.sum(chosen * places[None, :].astype(jnp.float32), axis=1).astype(jnp.int32)
    live = jnp.dot(jnp.dot(arrange, mask), pick.T)
    upper = (places[:, None] <= places[None, :]).astype(jnp.float32)
    rank = jnp.dot(live, upper).astype(jnp.int32) - 1
    counts = rank[:, -1] + 1
    hit = (rank[:, :, None] == places[None, None, :]) & (live[:, :, None] > 0.5)
    listed = jnp.sum(jnp.where(hit, places[None, :, None], 0), axis=1)
    used = places[None, :] < counts[:, None]
    key_list = jnp.where(used, listed, listed[:, :1]).reshape(-1)
    value_list = jnp.where(used, listed, tiles).reshape(-1)
    counts = jnp.concatenate([counts, active.astype(jnp.int32)[None]])
    return order, key_list, value_list, counts


def head_slot(head):
    return head + head // 3


def sync_peers(here, peers):
    barrier = pltpu.get_barrier_semaphore()
    for peer in peers:
        pl.semaphore_signal(barrier, inc=1, device_id=peer, device_id_type=MESH)
    pl.semaphore_wait(barrier, len(peers))


def whereabouts(groups, ring):
    ctx, head, part = lax.axis_index("ctx"), lax.axis_index("head"), lax.axis_index("dp")
    shift = lax.rem(part, 2)
    right, left = lax.rem(head + 1, ring), lax.rem(head + ring - 1, ring)
    peers = [(ctx, left, part), (ctx, right, part)]
    peers += [(lax.rem(ctx + i, groups), head, part) for i in range(1, groups)]
    active = lax.rem(ctx + groups - shift, 4) != 3
    return ctx, head, part, shift, right, left, peers, active


def front_kernel(
    groups, ring, heads, patch_ref, wq_ref, wk_ref, wv_ref, out_ref,
    rows_all, weights, stage, weight_sem, own_sem, left_sem, right_sem, pass_sem, far_sem,
    give_sem, self_sem, take_sem,
):
    tokens, width = patch_ref.shape
    chunk = FRONT_ROWS
    chunks = tokens // chunk
    ctx, head, part, shift, right, left, peers, active = whereabouts(groups, ring)
    across = lax.rem(head + 2, ring)

    loads = [
        pltpu.make_async_copy(ref, weights.at[i], weight_sem.at[i])
        for i, ref in enumerate((wq_ref, wk_ref, wv_ref))
    ]
    for load in loads:
        load.start()
    sync_peers(ctx, peers)

    def span(c):
        return pl.ds(pl.multiple_of(c * chunk, chunk), chunk)

    def own_copy(c, way, to, sems):
        return pltpu.make_async_remote_copy(
            src_ref=patch_ref.at[span(c), :],
            dst_ref=rows_all.at[head, span(c), :],
            send_sem=own_sem.at[way, c],
            recv_sem=sems.at[c],
            device_id=(ctx, to, part),
            device_id_type=MESH,
        )

    def arrival(slot, c, sems):
        return pltpu.make_async_copy(
            rows_all.at[slot, span(c), :], rows_all.at[slot, span(c), :], sems.at[c]
        )

    def send_own(c):
        own_copy(c, 0, right, left_sem).start()
        own_copy(c, 1, left, right_sem).start()

    def pass_copy(c, slot, to):
        return pltpu.make_async_remote_copy(
            src_ref=rows_all.at[slot, span(c), :],
            dst_ref=rows_all.at[slot, span(c), :],
            send_sem=pass_sem.at[c],
            recv_sem=far_sem.at[c],
            device_id=(ctx, to, part),
            device_id_type=MESH,
        )

    def give_copy(c, h):
        target = lax.rem(head_slot(h) + shift, groups)
        return target, pltpu.make_async_remote_copy(
            src_ref=stage.at[h, span(c), :],
            dst_ref=out_ref.at[ctx, span(c), :],
            send_sem=give_sem.at[h, c],
            recv_sem=take_sem,
            device_id=(target, head, part),
            device_id_type=MESH,
        )

    def keep_copy(c, h):
        return pltpu.make_async_copy(
            stage.at[h, span(c), :], out_ref.at[ctx, span(c), :], self_sem.at[c]
        )

    def project_chunk(c):
        for pair in range(heads // 2):
            cols = slice(pair * 2 * HDIM, (pair + 1) * 2 * HDIM)
            for i in range(3):
                total = jnp.dot(
                    rows_all[0, span(c), :], weights[i, :width, cols],
                    preferred_element_type=jnp.float32,
                )
                for k in range(1, ring):
                    total += jnp.dot(
                        rows_all[k, span(c), :], weights[i, k * width : (k + 1) * width, cols],
                        preferred_element_type=jnp.float32,
                    )
                total = total.astype(jnp.bfloat16)
                for j in range(2):
                    stage[2 * pair + j, span(c), i * HDIM : (i + 1) * HDIM] = total[
                        :, j * HDIM : (j + 1) * HDIM
                    ]
            for j in range(2):
                h = 2 * pair + j
                target, copy = give_copy(c, h)

                @pl.when(target != ctx)
                def _():
                    copy.start()

                @pl.when(target == ctx)
                def _():
                    keep_copy(c, h).start()

    ahead = min(FRONT_AHEAD, chunks)
    for c in range(ahead):
        send_own(c)
    rows_all[head] = patch_ref[...]
    for load in loads:
        load.wait()

    def step(c, carry):
        @pl.when(c < chunks)
        def _():
            arrival(left, c, left_sem).wait()
            arrival(right, c, right_sem).wait()

            @pl.when(lax.rem(c, 2) == 0)
            def _():
                pass_copy(c, left, right).start()

            @pl.when(lax.rem(c, 2) == 1)
            def _():
                pass_copy(c, right, left).start()

        @pl.when(c + ahead < chunks)
        def _():
            send_own(c + ahead)

        @pl.when(c > 0)
        def _():
            arrival(across, c - 1, far_sem).wait()
            project_chunk(c - 1)

        return carry

    lax.fori_loop(0, chunks + 1, step, 0)

    def settle(c, carry):
        own_copy(c, 0, right, left_sem).wait_send()
        own_copy(c, 1, left, right_sem).wait_send()
        pass_copy(c, left, right).wait_send()
        for h in range(heads):
            target, copy = give_copy(c, h)

            @pl.when(target != ctx)
            def _():
                copy.wait_send()

            @pl.when(target == ctx)
            def _():
                keep_copy(c, h).wait()

        return carry

    lax.fori_loop(0, chunks, settle, 0)

    @pl.when(active)
    def _():
        others = pl.ds(0, groups - 1)
        pltpu.make_async_copy(out_ref.at[others], out_ref.at[others], take_sem).wait()


def front(groups, ring, patch_rows, query_weight, key_weight, value_weight):
    tokens, width = patch_rows.shape
    depth, columns = query_weight.shape
    heads = columns // HDIM
    chunks = tokens // FRONT_ROWS
    dma = pltpu.SemaphoreType.DMA
    return pl.pallas_call(
        functools.partial(front_kernel, groups, ring, heads),
        out_shape=jax.ShapeDtypeStruct((groups, tokens, 3 * HDIM), jnp.bfloat16),
        in_specs=[pl.BlockSpec(memory_space=pltpu.VMEM)] + [pl.BlockSpec(memory_space=pl.ANY)] * 3,
        out_specs=pl.BlockSpec(memory_space=pl.ANY),
        scratch_shapes=[
            pltpu.VMEM((ring, tokens, width), jnp.bfloat16),
            pltpu.VMEM((3, depth, columns), jnp.bfloat16),
            pltpu.VMEM((heads, tokens, 3 * HDIM), jnp.bfloat16),
            dma((3,)),
            dma((2, chunks)),
            dma((chunks,)),
            dma((chunks,)),
            dma((chunks,)),
            dma((chunks,)),
            dma((heads, chunks)),
            dma((chunks,)),
            dma,
        ],
        compiler_params=pltpu.CompilerParams(
            collective_id=0, has_side_effects=True, vmem_limit_bytes=40 * 1024 * 1024
        ),
        cost_estimate=pl.CostEstimate(
            flops=6 * tokens * depth * columns, bytes_accessed=8 * depth * columns, transcendentals=0
        ),
        name="front",
    )(patch_rows, query_weight, key_weight, value_weight)


def body(patch_rows, query_weight, key_weight, value_weight, output_weight, tile_slot, tile_mask):
    groups = lax.axis_size("ctx")
    shard = lax.axis_index("ctx")
    tokens = patch_rows.shape[0]
    ring = lax.axis_size("head")
    heads = query_weight.shape[1] // HDIM
    shift = lax.rem(lax.axis_index("dp"), 2)
    active = lax.rem(shard + groups - shift, 4) != 3
    order, key_list, value_list, counts = live_lists(tile_slot, tile_mask, active)
    sent = front(groups, ring, patch_rows, query_weight, key_weight, value_weight)
    attended = attend(order, key_list, value_list, counts, sent.reshape(groups * tokens, 3 * HDIM))
    back = lax.all_to_all(
        attended.reshape(groups, tokens, HDIM), "ctx", split_axis=0, concat_axis=0, tiled=True
    )
    back = jnp.roll(back, -shift, axis=0)
    attended = jnp.concatenate([back[head_slot(h)] for h in range(heads)], axis=1)
    partial_out = jnp.dot(attended, output_weight, preferred_element_type=jnp.float32)
    return lax.psum_scatter(
        partial_out.astype(jnp.bfloat16), "head", scatter_dimension=1, tiled=True
    )


def solution(mesh):
    in_specs = (
        P(("dp", "ctx"), "head"),
        P(None, "head"),
        P(None, "head"),
        P(None, "head"),
        P("head", None),
        P("dp"),
        P("dp", None),
    )
    out_specs = P(("dp", "ctx"), "head")
    return jax.shard_map(body, mesh=mesh, in_specs=in_specs, out_specs=out_specs, check_vma=False)
```

```python
import functools
import math

import jax
import jax.numpy as jnp
from jax import lax
from jax.experimental import pallas as pl
from jax.experimental.pallas import tpu as pltpu
from jax.sharding import PartitionSpec as P

HDIM = 128
TILE = 128
GROUP = 8
TOGETHER = 3
FRONT_ROWS = 128
FRONT_AHEAD = 2
BACK_ROWS = 128
MESH = pl.DeviceIdType.MESH
LOG2E = 1.4426950408889634


def attend_kernel(
    order, key_list, value_list, counts, qkv_ref, out_ref, keys_t, values, scores
):
    tiles = qkv_ref.shape[0] // TILE
    pad = key_list.shape[0] // tiles
    stages = tiles // TOGETHER
    factor = LOG2E / math.sqrt(HDIM)

    def at(tile):
        return pl.ds(pl.multiple_of(tile * TILE, TILE), TILE)

    def score_step(queries, stage, g, peaks):
        fresh = []
        for j in range(TOGETHER):
            base = (stage * TOGETHER + j) * pad + g * GROUP
            peak = peaks[j]
            for i in range(0, GROUP, 2):
                block = jnp.concatenate(
                    [keys_t[:, at(key_list[base + i])], keys_t[:, at(key_list[base + i + 1])]], axis=1
                )
                found = jnp.dot(queries[j], block, preferred_element_type=jnp.float32)
                scores[lax.rem(stage, 2), g, j, :, i * TILE : (i + 2) * TILE] = found
                peak = jnp.maximum(peak, jnp.maximum(found[:, :TILE], found[:, TILE:]))
            fresh.append(peak)
        return tuple(fresh)

    def value_step(stage, g, row_peaks, totals):
        fresh = []
        for j in range(TOGETHER):
            base = (stage * TOGETHER + j) * pad + g * GROUP
            weight = jnp.exp2(
                scores[lax.rem(stage, 2), g, j] * factor - row_peaks[j]
            ).astype(jnp.bfloat16)
            block = jnp.concatenate([values[at(value_list[base + i]), :] for i in range(GROUP)], axis=0)
            fresh.append(totals[j] + jnp.dot(weight, block, preferred_element_type=jnp.float32))
        return tuple(fresh)

    def load_queries(stage):
        return [qkv_ref[at(order[stage * TOGETHER + j]), :HDIM] for j in range(TOGETHER)]

    def steps_of(stage):
        return (counts[stage * TOGETHER] + GROUP - 1) // GROUP

    def to_rows(peaks):
        return tuple(
            jnp.broadcast_to(jnp.max(peak, axis=1, keepdims=True) * factor, (TILE, 1)) for peak in peaks
        )

    def finish(stage, totals):
        for j in range(TOGETHER):
            out_ref[at(order[stage * TOGETHER + j]), :] = (
                totals[j][:, :HDIM] / totals[j][:, HDIM:]
            ).astype(jnp.bfloat16)

    low = tuple(jnp.full((TILE, TILE), -jnp.inf, jnp.float32) for _ in range(TOGETHER))
    zero = tuple(jnp.zeros((TILE, 2 * HDIM), jnp.float32) for _ in range(TOGETHER))

    @pl.when(counts[tiles] == 1)
    def _():
        def prepare(t, carry):
            keys_t[:, at(t)] = qkv_ref[at(t), HDIM : 2 * HDIM].T
            values[at(t), :HDIM] = qkv_ref[at(t), 2 * HDIM :]
            values[at(t), HDIM:] = jnp.ones((TILE, HDIM), jnp.bfloat16)
            return carry

        lax.fori_loop(0, tiles, prepare, 0, unroll=2)
        values[pl.ds(tiles * TILE, TILE), :] = jnp.zeros((TILE, 2 * HDIM), jnp.bfloat16)

        queries = load_queries(0)
        peaks = lax.fori_loop(0, steps_of(0), lambda g, p: score_step(queries, 0, g, p), low)

        def stage_body(stage, row_peaks):
            queries = load_queries(stage)

            def both(g, carry):
                peaks, totals = carry
                totals = value_step(stage - 1, g, row_peaks, totals)
                peaks = score_step(queries, stage, g, peaks)
                return peaks, totals

            peaks, totals = lax.fori_loop(0, steps_of(stage - 1), both, (low, zero))
            finish(stage - 1, totals)
            return to_rows(peaks)

        row_peaks = lax.fori_loop(1, stages, stage_body, to_rows(peaks))
        totals = lax.fori_loop(
            0, steps_of(stages - 1), lambda g, t: value_step(stages - 1, g, row_peaks, t), zero
        )
        finish(stages - 1, totals)


def attend(order, key_list, value_list, counts, qkv):
    rows = qkv.shape[0]
    return pl.pallas_call(
        attend_kernel,
        out_shape=jax.ShapeDtypeStruct((rows, HDIM), jnp.bfloat16),
        grid_spec=pltpu.PrefetchScalarGridSpec(
            num_scalar_prefetch=4,
            grid=(1,),
            in_specs=[pl.BlockSpec((rows, 3 * HDIM), lambda i, *_: (0, 0))],
            out_specs=pl.BlockSpec((rows, HDIM), lambda i, *_: (0, 0)),
            scratch_shapes=[
                pltpu.VMEM((HDIM, rows), jnp.bfloat16),
                pltpu.VMEM((rows + TILE, 2 * HDIM), jnp.bfloat16),
                pltpu.VMEM(
                    (2, rows // (TILE * GROUP), TOGETHER, TILE, GROUP * TILE), jnp.float32
                ),
            ],
        ),
        compiler_params=pltpu.CompilerParams(vmem_limit_bytes=52 * 1024 * 1024),
        cost_estimate=pl.CostEstimate(
            flops=4 * rows * rows * HDIM, bytes_accessed=8 * rows * HDIM, transcendentals=rows * rows
        ),
        name="attend",
    )(order, key_list, value_list, counts, qkv)


def live_lists(tile_slot, tile_mask, active):
    tiles = tile_slot.shape[0]
    places = jnp.arange(tiles, dtype=jnp.int32)
    pick = (tile_slot[:, None] == places[None, :]).astype(jnp.float32)
    mask = (tile_mask == 1).astype(jnp.float32)
    size = jnp.sum(mask, axis=1)
    ahead = (size[None, :] > size[:, None]) | (
        (size[None, :] == size[:, None]) & (places[None, :] < places[:, None])
    )
    position = jnp.sum(ahead.astype(jnp.int32), axis=1)
    arrange = (position[None, :] == places[:, None]).astype(jnp.float32)
    chosen = jnp.dot(arrange, pick.T)
    order = jnp.sum(chosen * places[None, :].astype(jnp.float32), axis=1).astype(jnp.int32)
    live = jnp.dot(jnp.dot(arrange, mask), pick.T)
    upper = (places[:, None] <= places[None, :]).astype(jnp.float32)
    rank = jnp.dot(live, upper).astype(jnp.int32) - 1
    counts = rank[:, -1] + 1
    hit = (rank[:, :, None] == places[None, None, :]) & (live[:, :, None] > 0.5)
    listed = jnp.sum(jnp.where(hit, places[None, :, None], 0), axis=1)
    used = places[None, :] < counts[:, None]
    key_list = jnp.where(used, listed, listed[:, :1]).reshape(-1)
    value_list = jnp.where(used, listed, tiles).reshape(-1)
    counts = jnp.concatenate([counts, active.astype(jnp.int32)[None]])
    return order, key_list, value_list, counts


def head_slot(head):
    return head + head // 3


def sync_peers(here, peers):
    barrier = pltpu.get_barrier_semaphore()
    for peer in peers:
        pl.semaphore_signal(barrier, inc=1, device_id=peer, device_id_type=MESH)
    pl.semaphore_wait(barrier, len(peers))


def whereabouts(groups, ring):
    ctx, head, part = lax.axis_index("ctx"), lax.axis_index("head"), lax.axis_index("dp")
    shift = lax.rem(part, 2)
    right, left = lax.rem(head + 1, ring), lax.rem(head + ring - 1, ring)
    peers = [(ctx, left, part), (ctx, right, part)]
    peers += [(lax.rem(ctx + i, groups), head, part) for i in range(1, groups)]
    active = lax.rem(ctx + groups - shift, 4) != 3
    return ctx, head, part, shift, right, left, peers, active


def front_kernel(
    groups, ring, heads, patch_ref, wq_ref, wk_ref, wv_ref, out_ref,
    rows_all, weights, stage, weight_sem, own_sem, left_sem, right_sem, pass_sem, far_sem,
    give_sem, self_sem, take_sem,
):
    tokens, width = patch_ref.shape
    chunk = FRONT_ROWS
    chunks = tokens // chunk
    ctx, head, part, shift, right, left, peers, active = whereabouts(groups, ring)
    across = lax.rem(head + 2, ring)

    loads = [
        pltpu.make_async_copy(ref, weights.at[i], weight_sem.at[i])
        for i, ref in enumerate((wq_ref, wk_ref, wv_ref))
    ]
    for load in loads:
        load.start()
    sync_peers(ctx, peers)

    def span(c):
        return pl.ds(pl.multiple_of(c * chunk, chunk), chunk)

    def own_copy(c, way, to, sems):
        return pltpu.make_async_remote_copy(
            src_ref=patch_ref.at[span(c), :],
            dst_ref=rows_all.at[head, span(c), :],
            send_sem=own_sem.at[way, c],
            recv_sem=sems.at[c],
            device_id=(ctx, to, part),
            device_id_type=MESH,
        )

    def arrival(slot, c, sems):
        return pltpu.make_async_copy(
            rows_all.at[slot, span(c), :], rows_all.at[slot, span(c), :], sems.at[c]
        )

    def send_own(c):
        own_copy(c, 0, right, left_sem).start()
        own_copy(c, 1, left, right_sem).start()

    def pass_copy(c, slot, to):
        return pltpu.make_async_remote_copy(
            src_ref=rows_all.at[slot, span(c), :],
            dst_ref=rows_all.at[slot, span(c), :],
            send_sem=pass_sem.at[c],
            recv_sem=far_sem.at[c],
            device_id=(ctx, to, part),
            device_id_type=MESH,
        )

    def give_copy(c, h):
        target = lax.rem(head_slot(h) + shift, groups)
        return target, pltpu.make_async_remote_copy(
            src_ref=stage.at[h, span(c), :],
            dst_ref=out_ref.at[ctx, span(c), :],
            send_sem=give_sem.at[h, c],
            recv_sem=take_sem,
            device_id=(target, head, part),
            device_id_type=MESH,
        )

    def keep_copy(c, h):
        return pltpu.make_async_copy(
            stage.at[h, span(c), :], out_ref.at[ctx, span(c), :], self_sem.at[c]
        )

    def project_chunk(c):
        for pair in range(heads // 2):
            cols = slice(pair * 2 * HDIM, (pair + 1) * 2 * HDIM)
            for i in range(3):
                total = jnp.dot(
                    rows_all[0, span(c), :], weights[i, :width, cols],
                    preferred_element_type=jnp.float32,
                )
                for k in range(1, ring):
                    total += jnp.dot(
                        rows_all[k, span(c), :], weights[i, k * width : (k + 1) * width, cols],
                        preferred_element_type=jnp.float32,
                    )
                total = total.astype(jnp.bfloat16)
                for j in range(2):
                    stage[2 * pair + j, span(c), i * HDIM : (i + 1) * HDIM] = total[
                        :, j * HDIM : (j + 1) * HDIM
                    ]
            for j in range(2):
                h = 2 * pair + j
                target, copy = give_copy(c, h)

                @pl.when(target != ctx)
                def _():
                    copy.start()

                @pl.when(target == ctx)
                def _():
                    keep_copy(c, h).start()

    ahead = min(FRONT_AHEAD, chunks)
    for c in range(ahead):
        send_own(c)
    rows_all[head] = patch_ref[...]
    for load in loads:
        load.wait()

    def step(c, carry):
        @pl.when(c < chunks)
        def _():
            arrival(left, c, left_sem).wait()
            arrival(right, c, right_sem).wait()

            @pl.when(lax.rem(c, 2) == 0)
            def _():
                pass_copy(c, left, right).start()

            @pl.when(lax.rem(c, 2) == 1)
            def _():
                pass_copy(c, right, left).start()

        @pl.when(c + ahead < chunks)
        def _():
            send_own(c + ahead)

        @pl.when(c > 0)
        def _():
            arrival(across, c - 1, far_sem).wait()
            project_chunk(c - 1)

        return carry

    lax.fori_loop(0, chunks + 1, step, 0)

    def settle(c, carry):
        own_copy(c, 0, right, left_sem).wait_send()
        own_copy(c, 1, left, right_sem).wait_send()
        pass_copy(c, left, right).wait_send()
        for h in range(heads):
            target, copy = give_copy(c, h)

            @pl.when(target != ctx)
            def _():
                copy.wait_send()

            @pl.when(target == ctx)
            def _():
                keep_copy(c, h).wait()

        return carry

    lax.fori_loop(0, chunks, settle, 0)

    @pl.when(active)
    def _():
        others = pl.ds(0, groups - 1)
        pltpu.make_async_copy(out_ref.at[others], out_ref.at[others], take_sem).wait()


def front(groups, ring, patch_rows, query_weight, key_weight, value_weight):
    tokens, width = patch_rows.shape
    depth, columns = query_weight.shape
    heads = columns // HDIM
    chunks = tokens // FRONT_ROWS
    dma = pltpu.SemaphoreType.DMA
    return pl.pallas_call(
        functools.partial(front_kernel, groups, ring, heads),
        out_shape=jax.ShapeDtypeStruct((groups, tokens, 3 * HDIM), jnp.bfloat16),
        in_specs=[pl.BlockSpec(memory_space=pltpu.VMEM)] + [pl.BlockSpec(memory_space=pl.ANY)] * 3,
        out_specs=pl.BlockSpec(memory_space=pl.ANY),
        scratch_shapes=[
            pltpu.VMEM((ring, tokens, width), jnp.bfloat16),
            pltpu.VMEM((3, depth, columns), jnp.bfloat16),
            pltpu.VMEM((heads, tokens, 3 * HDIM), jnp.bfloat16),
            dma((3,)),
            dma((2, chunks)),
            dma((chunks,)),
            dma((chunks,)),
            dma((chunks,)),
            dma((chunks,)),
            dma((heads, chunks)),
            dma((chunks,)),
            dma,
        ],
        compiler_params=pltpu.CompilerParams(
            collective_id=0, has_side_effects=True, vmem_limit_bytes=40 * 1024 * 1024
        ),
        cost_estimate=pl.CostEstimate(
            flops=6 * tokens * depth * columns, bytes_accessed=8 * depth * columns, transcendentals=0
        ),
        name="front",
    )(patch_rows, query_weight, key_weight, value_weight)


def back_kernel(
    groups, ring, heads, att_ref, wo_ref, out_ref,
    gathered, weights, far_out, far_in, side_out, side_in, own, pending,
    weight_sem, give_sem, self_sem, take_sem, far_send, far_recv, side_send, side_recv,
):
    tokens, width = out_ref.shape
    chunk = BACK_ROWS
    chunks = tokens // chunk
    ctx, head, part, shift, right, left, peers, active = whereabouts(groups, ring)
    across = lax.rem(head + 2, ring)
    unit = lax.rem(ctx + groups - shift, groups)
    mine = jnp.minimum(unit - unit // 4, heads - 1)

    loads = [
        pltpu.make_async_copy(
            wo_ref.at[:, pl.ds(pl.multiple_of(block * width, width), width)],
            weights.at[i],
            weight_sem.at[i],
        )
        for i, block in enumerate((across, right, left, head))
    ]
    for load in loads:
        load.start()
    sync_peers(ctx, peers)

    def span(c):
        return pl.ds(pl.multiple_of(c * chunk, chunk), chunk)

    def give_copy(c, i):
        source = lax.rem(ctx + i, groups)
        return pltpu.make_async_remote_copy(
            src_ref=att_ref.at[source, span(c), :],
            dst_ref=gathered.at[mine, span(c), :],
            send_sem=give_sem.at[i - 1, c],
            recv_sem=take_sem.at[c],
            device_id=(source, head, part),
            device_id_type=MESH,
        )

    def keep_copy(c):
        return pltpu.make_async_copy(
            att_ref.at[ctx, span(c), :], gathered.at[mine, span(c), :], self_sem.at[c]
        )

    @pl.when(active)
    def _():
        def give(c, carry):
            keep_copy(c).start()
            for i in range(1, groups):
                give_copy(c, i).start()
            return carry

        lax.fori_loop(0, chunks, give, 0)

    def far_copy(c, to):
        return pltpu.make_async_remote_copy(
            src_ref=far_out.at[span(c), :],
            dst_ref=far_in.at[span(c), :],
            send_sem=far_send.at[c],
            recv_sem=far_recv.at[c],
            device_id=(ctx, to, part),
            device_id_type=MESH,
        )

    def side_copy(c, way, to):
        return pltpu.make_async_remote_copy(
            src_ref=side_out.at[way, span(c), :],
            dst_ref=side_in.at[way, span(c), :],
            send_sem=side_send.at[way, c],
            recv_sem=side_recv.at[way, c],
            device_id=(ctx, to, part),
            device_id_type=MESH,
        )

    for load in loads:
        load.wait()

    def mix(c):
        @pl.when(active)
        def _():
            keep_copy(c).wait()
            others = pl.ds(0, heads - 1)
            pltpu.make_async_copy(
                gathered.at[others, span(c), :], gathered.at[others, span(c), :], take_sem.at[c]
            ).wait()

        @pl.when(jnp.logical_not(active))
        def _():
            pltpu.make_async_copy(
                gathered.at[:, span(c), :], gathered.at[:, span(c), :], take_sem.at[c]
            ).wait()

        rows = jnp.concatenate([gathered[h, span(c), :] for h in range(heads)], axis=1)

        def part_sum(i):
            return jnp.dot(rows, weights[i], preferred_element_type=jnp.float32)

        far_out[span(c), :] = part_sum(0).astype(jnp.bfloat16)
        even = lax.rem(c, 2) == 0

        @pl.when(even)
        def _():
            far_copy(c, right).start()
            side_out[1, span(c), :] = part_sum(2).astype(jnp.bfloat16)
            side_copy(c, 1, left).start()
            pending[span(c), :] = part_sum(1)

        @pl.when(jnp.logical_not(even))
        def _():
            far_copy(c, left).start()
            side_out[0, span(c), :] = part_sum(1).astype(jnp.bfloat16)
            side_copy(c, 0, right).start()
            pending[span(c), :] = part_sum(2)

        own[span(c), :] = part_sum(3)

    def merge(c):
        far_copy(c, right).wait_recv()
        merged = (pending[span(c), :] + far_in[span(c), :].astype(jnp.float32)).astype(jnp.bfloat16)
        even = lax.rem(c, 2) == 0

        @pl.when(even)
        def _():
            side_out[0, span(c), :] = merged
            side_copy(c, 0, right).start()

        @pl.when(jnp.logical_not(even))
        def _():
            side_out[1, span(c), :] = merged
            side_copy(c, 1, left).start()

    def close(c):
        side_copy(c, 0, right).wait_recv()
        side_copy(c, 1, left).wait_recv()
        out_ref[span(c), :] = (
            own[span(c), :]
            + side_in[0, span(c), :].astype(jnp.float32)
            + side_in[1, span(c), :].astype(jnp.float32)
        ).astype(jnp.bfloat16)

    def step(c, carry):
        @pl.when((c > 0) & (c <= chunks))
        def _():
            merge(c - 1)

        @pl.when(c < chunks)
        def _():
            mix(c)

        @pl.when(c > 1)
        def _():
            close(c - 2)

        return carry

    lax.fori_loop(0, chunks + 2, step, 0)

    def settle(c, carry):
        far_copy(c, right).wait_send()
        side_copy(c, 0, right).wait_send()
        side_copy(c, 1, left).wait_send()

        @pl.when(active)
        def _():
            for i in range(1, groups):
                give_copy(c, i).wait_send()

        return carry

    lax.fori_loop(0, chunks, settle, 0)


def back(groups, ring, attended, output_weight):
    tokens = attended.shape[1]
    columns, depth = output_weight.shape
    width = depth // ring
    heads = columns // HDIM
    chunks = tokens // BACK_ROWS
    dma = pltpu.SemaphoreType.DMA
    return pl.pallas_call(
        functools.partial(back_kernel, groups, ring, heads),
        out_shape=jax.ShapeDtypeStruct((tokens, width), jnp.bfloat16),
        in_specs=[pl.BlockSpec(memory_space=pl.ANY)] * 2,
        out_specs=pl.BlockSpec(memory_space=pltpu.VMEM),
        scratch_shapes=[
            pltpu.VMEM((heads, tokens, HDIM), jnp.bfloat16),
            pltpu.VMEM((ring, columns, width), jnp.bfloat16),
            pltpu.VMEM((tokens, width), jnp.bfloat16),
            pltpu.VMEM((tokens, width), jnp.bfloat16),
            pltpu.VMEM((2, tokens, width), jnp.bfloat16),
            pltpu.VMEM((2, tokens, width), jnp.bfloat16),
            pltpu.VMEM((tokens, width), jnp.float32),
            pltpu.VMEM((tokens, width), jnp.float32),
            dma((ring,)),
            dma((groups - 1, chunks)),
            dma((chunks,)),
            dma((chunks,)),
            dma((chunks,)),
            dma((chunks,)),
            dma((2, chunks)),
            dma((2, chunks)),
        ],
        compiler_params=pltpu.CompilerParams(
            collective_id=1, has_side_effects=True, vmem_limit_bytes=40 * 1024 * 1024
        ),
        cost_estimate=pl.CostEstimate(
            flops=2 * tokens * depth * columns, bytes_accessed=2 * depth * columns, transcendentals=0
        ),
        name="back",
    )(attended, output_weight)


def body(patch_rows, query_weight, key_weight, value_weight, output_weight, tile_slot, tile_mask):
    groups = lax.axis_size("ctx")
    shard = lax.axis_index("ctx")
    tokens = patch_rows.shape[0]
    ring = lax.axis_size("head")
    heads = query_weight.shape[1] // HDIM
    shift = lax.rem(lax.axis_index("dp"), 2)
    active = lax.rem(shard + groups - shift, 4) != 3
    order, key_list, value_list, counts = live_lists(tile_slot, tile_mask, active)
    sent = front(groups, ring, patch_rows, query_weight, key_weight, value_weight)
    attended = attend(order, key_list, value_list, counts, sent.reshape(groups * tokens, 3 * HDIM))
    return back(groups, ring, attended.reshape(groups, tokens, HDIM), output_weight)


def solution(mesh):
    in_specs = (
        P(("dp", "ctx"), "head"),
        P(None, "head"),
        P(None, "head"),
        P(None, "head"),
        P("head", None),
        P("dp"),
        P("dp", None),
    )
    out_specs = P(("dp", "ctx"), "head")
    return jax.shard_map(body, mesh=mesh, in_specs=in_specs, out_specs=out_specs, check_vma=False)
```

```python
import functools
import math

import jax
import jax.numpy as jnp
from jax import lax
from jax.experimental import pallas as pl
from jax.experimental.pallas import tpu as pltpu
from jax.sharding import PartitionSpec as P

HDIM = 128
TILE = 128
GROUP = 8
TOGETHER = 3
WIDE = 2
FRONT_ROWS = 128
FRONT_AHEAD = 2
BACK_ROWS = 128
MESH = pl.DeviceIdType.MESH
LOG2E = 1.4426950408889634


def attend_kernel(
    is_active, slot_ref, mask_ref, qkv_ref, out_ref,
    query_key, values, scores, plan_rows, plan, load_sem, plan_sem,
):
    tokens = out_ref.shape[0]
    tiles = tokens // TILE
    stages = tiles // TOGETHER
    factor = LOG2E / math.sqrt(HDIM)

    def at(tile):
        return pl.ds(pl.multiple_of(tile * TILE, TILE), TILE)

    def make_plan():
        def iota(shape, axis):
            return lax.broadcasted_iota(jnp.int32, shape, axis)

        def product(a, b, dims=((1,), (0,))):
            return lax.dot_general(a, b, (dims, ((), ())), preferred_element_type=jnp.float32)

        square = (tiles, tiles)
        row, col = iota(square, 0), iota(square, 1)
        home = (slot_ref[...] == row).astype(jnp.float32)
        mask = (mask_ref[...] == 1).astype(jnp.float32)
        size = jnp.sum(mask, axis=1, keepdims=True)
        size_row = product(jnp.ones((1, tiles), jnp.float32), mask, ((1,), (1,)))
        ahead = (size > size_row) | ((size == size_row) & (row < col))
        position = jnp.sum(ahead.astype(jnp.float32), axis=0, keepdims=True)
        arrange = (position == row.astype(jnp.float32)).astype(jnp.float32)
        chosen = product(arrange, home)
        order = jnp.sum(chosen * col.astype(jnp.float32), axis=1, keepdims=True)
        live = product(product(arrange, mask), home)
        rank = product(live, (row <= col).astype(jnp.float32))
        count = jnp.sum(live, axis=1, keepdims=True)
        rank = jnp.where(live > 0.5, rank - 1.0, -1.0)
        lane = iota((tiles, 128), 1).astype(jnp.float32)
        listed = jnp.zeros((tiles, 128), jnp.float32)
        for u in range(1, tiles):
            listed += jnp.where(rank[:, u : u + 1] == lane, float(u), 0.0)
        used = lane < count
        plan_rows[0] = jnp.where(used, listed, listed[:, :1]).astype(jnp.int32)
        plan_rows[1] = jnp.where(used, listed, float(tiles)).astype(jnp.int32)
        plan_rows[2] = jnp.where(lane == 0.0, order, count).astype(jnp.int32)
        move = pltpu.make_async_copy(plan_rows, plan, plan_sem)
        move.start()
        move.wait()

    def score_step(queries, stage, g, peaks):
        fresh = []
        for j in range(TOGETHER):
            r, base = stage * TOGETHER + j, g * GROUP
            peak = peaks[j]
            for i in range(0, GROUP, WIDE):
                block = jnp.concatenate(
                    [query_key[at(plan[0, r, base + i + k]), HDIM:] for k in range(WIDE)], axis=0
                )
                found = lax.dot_general(
                    queries[j], block, (((1,), (1,)), ((), ())), preferred_element_type=jnp.float32
                )
                scores[lax.rem(stage, 2), g, j, :, i * TILE : (i + WIDE) * TILE] = found
                for k in range(WIDE):
                    peak = jnp.maximum(peak, found[:, k * TILE : (k + 1) * TILE])
            fresh.append(peak)
        return tuple(fresh)

    def value_step(stage, g, row_peaks, totals):
        fresh = []
        for j in range(TOGETHER):
            r, base = stage * TOGETHER + j, g * GROUP
            weight = jnp.exp2(
                scores[lax.rem(stage, 2), g, j] * factor - row_peaks[j]
            ).astype(jnp.bfloat16)
            block = jnp.concatenate([values[at(plan[1, r, base + i]), :] for i in range(GROUP)], axis=0)
            fresh.append(totals[j] + jnp.dot(weight, block, preferred_element_type=jnp.float32))
        return tuple(fresh)

    def tile_of(stage, j):
        return plan[2, stage * TOGETHER + j, 0]

    def load_queries(stage):
        return [query_key[at(tile_of(stage, j)), :HDIM] for j in range(TOGETHER)]

    def steps_of(stage):
        return (plan[2, stage * TOGETHER, 1] + GROUP - 1) // GROUP

    def to_rows(peaks):
        return tuple(jnp.max(peak, axis=1, keepdims=True) * factor for peak in peaks)

    def finish(stage, totals):
        for j in range(TOGETHER):
            out_ref[at(tile_of(stage, j)), :] = (
                totals[j][:, :HDIM] / totals[j][:, HDIM:]
            ).astype(jnp.bfloat16)

    low = tuple(jnp.full((TILE, TILE), -jnp.inf, jnp.float32) for _ in range(TOGETHER))
    zero = tuple(jnp.zeros((TILE, 2 * HDIM), jnp.float32) for _ in range(TOGETHER))

    @pl.when(is_active())
    def _():
        loads = [
            pltpu.make_async_copy(qkv_ref.at[:, : 2 * HDIM], query_key, load_sem.at[0]),
            pltpu.make_async_copy(
                qkv_ref.at[:, 2 * HDIM :], values.at[pl.ds(0, tokens), pl.ds(0, HDIM)], load_sem.at[1]
            ),
        ]
        for load in loads:
            load.start()
        make_plan()
        values[pl.ds(0, tokens), HDIM:] = jnp.ones((tokens, HDIM), jnp.bfloat16)
        values[pl.ds(tokens, TILE), :] = jnp.zeros((TILE, 2 * HDIM), jnp.bfloat16)
        for load in loads:
            load.wait()

        queries = load_queries(0)
        peaks = lax.fori_loop(0, steps_of(0), lambda g, p: score_step(queries, 0, g, p), low)

        def stage_body(stage, row_peaks):
            queries = load_queries(stage)

            def both(g, carry):
                peaks, totals = carry
                totals = value_step(stage - 1, g, row_peaks, totals)
                peaks = score_step(queries, stage, g, peaks)
                return peaks, totals

            peaks, totals = lax.fori_loop(0, steps_of(stage - 1), both, (low, zero))
            finish(stage - 1, totals)
            return to_rows(peaks)

        row_peaks = lax.fori_loop(1, stages, stage_body, to_rows(peaks))
        totals = lax.fori_loop(
            0, steps_of(stages - 1), lambda g, t: value_step(stages - 1, g, row_peaks, t), zero
        )
        finish(stages - 1, totals)


def attend(is_active, tile_slot, tile_mask, qkv):
    rows = qkv.shape[0]
    tiles = rows // TILE
    return pl.pallas_call(
        functools.partial(attend_kernel, is_active),
        out_shape=jax.ShapeDtypeStruct((rows, HDIM), jnp.bfloat16),
        in_specs=[
            pl.BlockSpec(memory_space=pltpu.VMEM),
            pl.BlockSpec(memory_space=pltpu.VMEM),
            pl.BlockSpec(memory_space=pl.ANY),
        ],
        out_specs=pl.BlockSpec(memory_space=pltpu.VMEM),
        scratch_shapes=[
            pltpu.VMEM((rows, 2 * HDIM), jnp.bfloat16),
            pltpu.VMEM((rows + TILE, 2 * HDIM), jnp.bfloat16),
            pltpu.VMEM((2, -(-tiles // GROUP), TOGETHER, TILE, GROUP * TILE), jnp.float32),
            pltpu.VMEM((3, tiles, 128), jnp.int32),
            pltpu.SMEM((3, tiles, 128), jnp.int32),
            pltpu.SemaphoreType.DMA((2,)),
            pltpu.SemaphoreType.DMA,
        ],
        compiler_params=pltpu.CompilerParams(vmem_limit_bytes=60 * 1024 * 1024),
        cost_estimate=pl.CostEstimate(
            flops=4 * rows * rows * HDIM, bytes_accessed=8 * rows * HDIM, transcendentals=rows * rows
        ),
        name="attend",
    )(tile_slot.reshape(1, tiles), tile_mask, qkv)


def head_slot(head):
    return head + head // 3


def sync_peers(here, peers):
    barrier = pltpu.get_barrier_semaphore()
    for peer in peers:
        pl.semaphore_signal(barrier, inc=1, device_id=peer, device_id_type=MESH)
    pl.semaphore_wait(barrier, len(peers))


def whereabouts(groups, ring):
    ctx, head, part = lax.axis_index("ctx"), lax.axis_index("head"), lax.axis_index("dp")
    shift = lax.rem(part, 2)
    right, left = lax.rem(head + 1, ring), lax.rem(head + ring - 1, ring)
    peers = [(ctx, left, part), (ctx, right, part)]
    peers += [(lax.rem(ctx + i, groups), head, part) for i in range(1, groups)]
    active = lax.rem(ctx + groups - shift, 4) != 3
    return ctx, head, part, shift, right, left, peers, active


def front_kernel(
    groups, ring, heads, patch_ref, wq_ref, wk_ref, wv_ref, out_ref,
    rows_all, weights, stage, weight_sem, own_sem, left_sem, right_sem, pass_sem, far_sem,
    give_sem, self_sem, take_sem,
):
    tokens, width = patch_ref.shape
    chunk = FRONT_ROWS
    chunks = tokens // chunk
    ctx, head, part, shift, right, left, peers, active = whereabouts(groups, ring)
    across = lax.rem(head + 2, ring)

    loads = [
        pltpu.make_async_copy(ref, weights.at[i], weight_sem.at[i])
        for i, ref in enumerate((wq_ref, wk_ref, wv_ref))
    ]
    for load in loads:
        load.start()
    sync_peers(ctx, peers)

    def span(c):
        return pl.ds(pl.multiple_of(c * chunk, chunk), chunk)

    def own_copy(c, way, to, sems):
        return pltpu.make_async_remote_copy(
            src_ref=patch_ref.at[span(c), :],
            dst_ref=rows_all.at[head, span(c), :],
            send_sem=own_sem.at[way, c],
            recv_sem=sems.at[c],
            device_id=(ctx, to, part),
            device_id_type=MESH,
        )

    def arrival(slot, c, sems):
        return pltpu.make_async_copy(
            rows_all.at[slot, span(c), :], rows_all.at[slot, span(c), :], sems.at[c]
        )

    def send_own(c):
        own_copy(c, 0, right, left_sem).start()
        own_copy(c, 1, left, right_sem).start()

    def pass_copy(c, slot, to):
        return pltpu.make_async_remote_copy(
            src_ref=rows_all.at[slot, span(c), :],
            dst_ref=rows_all.at[slot, span(c), :],
            send_sem=pass_sem.at[c],
            recv_sem=far_sem.at[c],
            device_id=(ctx, to, part),
            device_id_type=MESH,
        )

    def give_copy(c, h):
        target = lax.rem(head_slot(h) + shift, groups)
        return target, pltpu.make_async_remote_copy(
            src_ref=stage.at[h, span(c), :],
            dst_ref=out_ref.at[ctx, span(c), :],
            send_sem=give_sem.at[h, c],
            recv_sem=take_sem,
            device_id=(target, head, part),
            device_id_type=MESH,
        )

    def keep_copy(c, h):
        return pltpu.make_async_copy(
            stage.at[h, span(c), :], out_ref.at[ctx, span(c), :], self_sem.at[c]
        )

    def project_chunk(c):
        for pair in range(heads // 2):
            cols = slice(pair * 2 * HDIM, (pair + 1) * 2 * HDIM)
            for i in range(3):
                total = jnp.dot(
                    rows_all[0, span(c), :], weights[i, :width, cols],
                    preferred_element_type=jnp.float32,
                )
                for k in range(1, ring):
                    total += jnp.dot(
                        rows_all[k, span(c), :], weights[i, k * width : (k + 1) * width, cols],
                        preferred_element_type=jnp.float32,
                    )
                total = total.astype(jnp.bfloat16)
                for j in range(2):
                    stage[2 * pair + j, span(c), i * HDIM : (i + 1) * HDIM] = total[
                        :, j * HDIM : (j + 1) * HDIM
                    ]
            for j in range(2):
                h = 2 * pair + j
                target, copy = give_copy(c, h)

                @pl.when(target != ctx)
                def _():
                    copy.start()

                @pl.when(target == ctx)
                def _():
                    keep_copy(c, h).start()

    ahead = min(FRONT_AHEAD, chunks)
    for c in range(ahead):
        send_own(c)
    rows_all[head] = patch_ref[...]
    for load in loads:
        load.wait()

    def step(c, carry):
        @pl.when(c < chunks)
        def _():
            arrival(left, c, left_sem).wait()
            arrival(right, c, right_sem).wait()

            @pl.when(lax.rem(c, 2) == 0)
            def _():
                pass_copy(c, left, right).start()

            @pl.when(lax.rem(c, 2) == 1)
            def _():
                pass_copy(c, right, left).start()

        @pl.when(c + ahead < chunks)
        def _():
            send_own(c + ahead)

        @pl.when(c > 0)
        def _():
            arrival(across, c - 1, far_sem).wait()
            project_chunk(c - 1)

        return carry

    lax.fori_loop(0, chunks + 1, step, 0)

    def settle(c, carry):
        own_copy(c, 0, right, left_sem).wait_send()
        own_copy(c, 1, left, right_sem).wait_send()
        pass_copy(c, left, right).wait_send()
        for h in range(heads):
            target, copy = give_copy(c, h)

            @pl.when(target != ctx)
            def _():
                copy.wait_send()

            @pl.when(target == ctx)
            def _():
                keep_copy(c, h).wait()

        return carry

    lax.fori_loop(0, chunks, settle, 0)

    @pl.when(active)
    def _():
        others = pl.ds(0, groups - 1)
        pltpu.make_async_copy(out_ref.at[others], out_ref.at[others], take_sem).wait()


def front(groups, ring, patch_rows, query_weight, key_weight, value_weight):
    tokens, width = patch_rows.shape
    depth, columns = query_weight.shape
    heads = columns // HDIM
    chunks = tokens // FRONT_ROWS
    dma = pltpu.SemaphoreType.DMA
    return pl.pallas_call(
        functools.partial(front_kernel, groups, ring, heads),
        out_shape=jax.ShapeDtypeStruct((groups, tokens, 3 * HDIM), jnp.bfloat16),
        in_specs=[pl.BlockSpec(memory_space=pltpu.VMEM)] + [pl.BlockSpec(memory_space=pl.ANY)] * 3,
        out_specs=pl.BlockSpec(memory_space=pl.ANY),
        scratch_shapes=[
            pltpu.VMEM((ring, tokens, width), jnp.bfloat16),
            pltpu.VMEM((3, depth, columns), jnp.bfloat16),
            pltpu.VMEM((heads, tokens, 3 * HDIM), jnp.bfloat16),
            dma((3,)),
            dma((2, chunks)),
            dma((chunks,)),
            dma((chunks,)),
            dma((chunks,)),
            dma((chunks,)),
            dma((heads, chunks)),
            dma((chunks,)),
            dma,
        ],
        compiler_params=pltpu.CompilerParams(
            collective_id=0, has_side_effects=True, vmem_limit_bytes=60 * 1024 * 1024
        ),
        cost_estimate=pl.CostEstimate(
            flops=6 * tokens * depth * columns, bytes_accessed=8 * depth * columns, transcendentals=0
        ),
        name="front",
    )(patch_rows, query_weight, key_weight, value_weight)


def back_kernel(
    groups, ring, heads, att_ref, wo_ref, out_ref,
    gathered, weights, far_out, far_in, side_out, side_in, own, pending,
    weight_sem, give_sem, self_sem, take_sem, far_send, far_recv, side_send, side_recv,
):
    tokens, width = out_ref.shape
    chunk = BACK_ROWS
    chunks = tokens // chunk
    ctx, head, part, shift, right, left, peers, active = whereabouts(groups, ring)
    across = lax.rem(head + 2, ring)
    unit = lax.rem(ctx + groups - shift, groups)
    mine = jnp.minimum(unit - unit // 4, heads - 1)

    loads = [
        pltpu.make_async_copy(
            wo_ref.at[:, pl.ds(pl.multiple_of(block * width, width), width)],
            weights.at[i],
            weight_sem.at[i],
        )
        for i, block in enumerate((across, right, left, head))
    ]
    for load in loads:
        load.start()
    sync_peers(ctx, peers)

    def span(c):
        return pl.ds(pl.multiple_of(c * chunk, chunk), chunk)

    def give_copy(c, i):
        source = lax.rem(ctx + i, groups)
        return pltpu.make_async_remote_copy(
            src_ref=att_ref.at[source, span(c), :],
            dst_ref=gathered.at[mine, span(c), :],
            send_sem=give_sem.at[i - 1, c],
            recv_sem=take_sem.at[c],
            device_id=(source, head, part),
            device_id_type=MESH,
        )

    def keep_copy(c):
        return pltpu.make_async_copy(
            att_ref.at[ctx, span(c), :], gathered.at[mine, span(c), :], self_sem.at[c]
        )

    @pl.when(active)
    def _():
        def give(c, carry):
            keep_copy(c).start()
            for i in range(1, groups):
                give_copy(c, i).start()
            return carry

        lax.fori_loop(0, chunks, give, 0)

    def far_copy(c, to):
        return pltpu.make_async_remote_copy(
            src_ref=far_out.at[span(c), :],
            dst_ref=far_in.at[span(c), :],
            send_sem=far_send.at[c],
            recv_sem=far_recv.at[c],
            device_id=(ctx, to, part),
            device_id_type=MESH,
        )

    def side_copy(c, way, to):
        return pltpu.make_async_remote_copy(
            src_ref=side_out.at[way, span(c), :],
            dst_ref=side_in.at[way, span(c), :],
            send_sem=side_send.at[way, c],
            recv_sem=side_recv.at[way, c],
            device_id=(ctx, to, part),
            device_id_type=MESH,
        )

    for load in loads:
        load.wait()

    def mix(c):
        @pl.when(active)
        def _():
            keep_copy(c).wait()
            others = pl.ds(0, heads - 1)
            pltpu.make_async_copy(
                gathered.at[others, span(c), :], gathered.at[others, span(c), :], take_sem.at[c]
            ).wait()

        @pl.when(jnp.logical_not(active))
        def _():
            pltpu.make_async_copy(
                gathered.at[:, span(c), :], gathered.at[:, span(c), :], take_sem.at[c]
            ).wait()

        rows = jnp.concatenate([gathered[h, span(c), :] for h in range(heads)], axis=1)

        def part_sum(i):
            return jnp.dot(rows, weights[i], preferred_element_type=jnp.float32)

        far_out[span(c), :] = part_sum(0).astype(jnp.bfloat16)
        even = lax.rem(c, 2) == 0

        @pl.when(even)
        def _():
            far_copy(c, right).start()
            side_out[1, span(c), :] = part_sum(2).astype(jnp.bfloat16)
            side_copy(c, 1, left).start()
            pending[span(c), :] = part_sum(1)

        @pl.when(jnp.logical_not(even))
        def _():
            far_copy(c, left).start()
            side_out[0, span(c), :] = part_sum(1).astype(jnp.bfloat16)
            side_copy(c, 0, right).start()
            pending[span(c), :] = part_sum(2)

        own[span(c), :] = part_sum(3)

    def merge(c):
        far_copy(c, right).wait_recv()
        merged = (pending[span(c), :] + far_in[span(c), :].astype(jnp.float32)).astype(jnp.bfloat16)
        even = lax.rem(c, 2) == 0

        @pl.when(even)
        def _():
            side_out[0, span(c), :] = merged
            side_copy(c, 0, right).start()

        @pl.when(jnp.logical_not(even))
        def _():
            side_out[1, span(c), :] = merged
            side_copy(c, 1, left).start()

    def close(c):
        side_copy(c, 0, right).wait_recv()
        side_copy(c, 1, left).wait_recv()
        out_ref[span(c), :] = (
            own[span(c), :]
            + side_in[0, span(c), :].astype(jnp.float32)
            + side_in[1, span(c), :].astype(jnp.float32)
        ).astype(jnp.bfloat16)

    def step(c, carry):
        @pl.when((c > 0) & (c <= chunks))
        def _():
            merge(c - 1)

        @pl.when(c < chunks)
        def _():
            mix(c)

        @pl.when(c > 1)
        def _():
            close(c - 2)

        return carry

    lax.fori_loop(0, chunks + 2, step, 0)

    def settle(c, carry):
        far_copy(c, right).wait_send()
        side_copy(c, 0, right).wait_send()
        side_copy(c, 1, left).wait_send()

        @pl.when(active)
        def _():
            for i in range(1, groups):
                give_copy(c, i).wait_send()

        return carry

    lax.fori_loop(0, chunks, settle, 0)


def back(groups, ring, attended, output_weight):
    tokens = attended.shape[1]
    columns, depth = output_weight.shape
    width = depth // ring
    heads = columns // HDIM
    chunks = tokens // BACK_ROWS
    dma = pltpu.SemaphoreType.DMA
    return pl.pallas_call(
        functools.partial(back_kernel, groups, ring, heads),
        out_shape=jax.ShapeDtypeStruct((tokens, width), jnp.bfloat16),
        in_specs=[pl.BlockSpec(memory_space=pl.ANY)] * 2,
        out_specs=pl.BlockSpec(memory_space=pltpu.VMEM),
        scratch_shapes=[
            pltpu.VMEM((heads, tokens, HDIM), jnp.bfloat16),
            pltpu.VMEM((ring, columns, width), jnp.bfloat16),
            pltpu.VMEM((tokens, width), jnp.bfloat16),
            pltpu.VMEM((tokens, width), jnp.bfloat16),
            pltpu.VMEM((2, tokens, width), jnp.bfloat16),
            pltpu.VMEM((2, tokens, width), jnp.bfloat16),
            pltpu.VMEM((tokens, width), jnp.float32),
            pltpu.VMEM((tokens, width), jnp.float32),
            dma((ring,)),
            dma((groups - 1, chunks)),
            dma((chunks,)),
            dma((chunks,)),
            dma((chunks,)),
            dma((chunks,)),
            dma((2, chunks)),
            dma((2, chunks)),
        ],
        compiler_params=pltpu.CompilerParams(
            collective_id=1, has_side_effects=True, vmem_limit_bytes=60 * 1024 * 1024
        ),
        cost_estimate=pl.CostEstimate(
            flops=2 * tokens * depth * columns, bytes_accessed=2 * depth * columns, transcendentals=0
        ),
        name="back",
    )(attended, output_weight)


def body(patch_rows, query_weight, key_weight, value_weight, output_weight, tile_slot, tile_mask):
    groups = lax.axis_size("ctx")
    tokens = patch_rows.shape[0]
    ring = lax.axis_size("head")
    sent = front(groups, ring, patch_rows, query_weight, key_weight, value_weight)

    def is_active():
        return whereabouts(groups, ring)[-1]

    attended = attend(is_active, tile_slot, tile_mask, sent.reshape(groups * tokens, 3 * HDIM))
    return back(groups, ring, attended.reshape(groups, tokens, HDIM), output_weight)


def solution(mesh):
    in_specs = (
        P(("dp", "ctx"), "head"),
        P(None, "head"),
        P(None, "head"),
        P(None, "head"),
        P("head", None),
        P("dp"),
        P("dp", None),
    )
    out_specs = P(("dp", "ctx"), "head")
    return jax.shard_map(body, mesh=mesh, in_specs=in_specs, out_specs=out_specs, check_vma=False)
```

```python
import functools
import math

import jax
import jax.numpy as jnp
from jax import lax
from jax.experimental import pallas as pl
from jax.experimental.pallas import tpu as pltpu
from jax.sharding import PartitionSpec as P

HDIM = 128
TILE = 128
GROUP = 8
TOGETHER = 3
WIDE = 2
FRONT_ROWS = 64
FRONT_AHEAD = 2
FRONT_LAG = 1
FRONT_ORDER = (1, 2, 3, 4, 5, 6, 7)
BACK_ROWS = 128
BACK_LAG = 2
MESH = pl.DeviceIdType.MESH
LOG2E = 1.4426950408889634


def attend_kernel(
    is_active, slot_ref, mask_ref, qkv_ref, out_ref,
    query_key, values, scores, plan_rows, plan, load_sem, plan_sem,
):
    tokens = out_ref.shape[0]
    tiles = tokens // TILE
    stages = tiles // TOGETHER
    factor = LOG2E / math.sqrt(HDIM)

    def at(tile):
        return pl.ds(pl.multiple_of(tile * TILE, TILE), TILE)

    def make_plan():
        def iota(shape, axis):
            return lax.broadcasted_iota(jnp.int32, shape, axis)

        def product(a, b, dims=((1,), (0,))):
            return lax.dot_general(a, b, (dims, ((), ())), preferred_element_type=jnp.float32)

        square = (tiles, tiles)
        row, col = iota(square, 0), iota(square, 1)
        home = (slot_ref[...] == row).astype(jnp.float32)
        mask = (mask_ref[...] == 1).astype(jnp.float32)
        size = jnp.sum(mask, axis=1, keepdims=True)
        size_row = product(jnp.ones((1, tiles), jnp.float32), mask, ((1,), (1,)))
        ahead = (size > size_row) | ((size == size_row) & (row < col))
        position = jnp.sum(ahead.astype(jnp.float32), axis=0, keepdims=True)
        arrange = (position == row.astype(jnp.float32)).astype(jnp.float32)
        chosen = product(arrange, home)
        order = jnp.sum(chosen * col.astype(jnp.float32), axis=1, keepdims=True)
        live = product(product(arrange, mask), home)
        rank = product(live, (row <= col).astype(jnp.float32))
        count = jnp.sum(live, axis=1, keepdims=True)
        rank = jnp.where(live > 0.5, rank - 1.0, -1.0)
        lane = iota((tiles, 128), 1).astype(jnp.float32)
        listed = jnp.zeros((tiles, 128), jnp.float32)
        for u in range(1, tiles):
            listed += jnp.where(rank[:, u : u + 1] == lane, float(u), 0.0)
        used = lane < count
        plan_rows[0] = jnp.where(used, listed, listed[:, :1]).astype(jnp.int32)
        plan_rows[1] = jnp.where(used, listed, float(tiles)).astype(jnp.int32)
        plan_rows[2] = jnp.where(lane == 0.0, order, count).astype(jnp.int32)
        move = pltpu.make_async_copy(plan_rows, plan, plan_sem)
        move.start()
        move.wait()

    def score_step(queries, stage, g, peaks):
        fresh = []
        for j in range(TOGETHER):
            r, base = stage * TOGETHER + j, g * GROUP
            peak = peaks[j]
            for i in range(0, GROUP, WIDE):
                block = jnp.concatenate(
                    [query_key[at(plan[0, r, base + i + k]), HDIM:] for k in range(WIDE)], axis=0
                )
                found = lax.dot_general(
                    queries[j], block, (((1,), (1,)), ((), ())), preferred_element_type=jnp.float32
                )
                scores[lax.rem(stage, 2), g, j, :, i * TILE : (i + WIDE) * TILE] = found
                for k in range(WIDE):
                    peak = jnp.maximum(peak, found[:, k * TILE : (k + 1) * TILE])
            fresh.append(peak)
        return tuple(fresh)

    def value_step(stage, g, row_peaks, totals):
        fresh = []
        for j in range(TOGETHER):
            r, base = stage * TOGETHER + j, g * GROUP
            weight = jnp.exp2(
                scores[lax.rem(stage, 2), g, j] * factor - row_peaks[j]
            ).astype(jnp.bfloat16)
            block = jnp.concatenate([values[at(plan[1, r, base + i]), :] for i in range(GROUP)], axis=0)
            fresh.append(totals[j] + jnp.dot(weight, block, preferred_element_type=jnp.float32))
        return tuple(fresh)

    def tile_of(stage, j):
        return plan[2, stage * TOGETHER + j, 0]

    def load_queries(stage):
        return [query_key[at(tile_of(stage, j)), :HDIM] for j in range(TOGETHER)]

    def steps_of(stage):
        return (plan[2, stage * TOGETHER, 1] + GROUP - 1) // GROUP

    def to_rows(peaks):
        return tuple(jnp.max(peak, axis=1, keepdims=True) * factor for peak in peaks)

    def finish(stage, totals):
        for j in range(TOGETHER):
            out_ref[at(tile_of(stage, j)), :] = (
                totals[j][:, :HDIM] / totals[j][:, HDIM:]
            ).astype(jnp.bfloat16)

    low = tuple(jnp.full((TILE, TILE), -jnp.inf, jnp.float32) for _ in range(TOGETHER))
    zero = tuple(jnp.zeros((TILE, 2 * HDIM), jnp.float32) for _ in range(TOGETHER))

    @pl.when(is_active())
    def _():
        loads = [
            pltpu.make_async_copy(qkv_ref.at[:, : 2 * HDIM], query_key, load_sem.at[0]),
            pltpu.make_async_copy(
                qkv_ref.at[:, 2 * HDIM :], values.at[pl.ds(0, tokens), pl.ds(0, HDIM)], load_sem.at[1]
            ),
        ]
        for load in loads:
            load.start()
        make_plan()
        values[pl.ds(0, tokens), HDIM:] = jnp.ones((tokens, HDIM), jnp.bfloat16)
        values[pl.ds(tokens, TILE), :] = jnp.zeros((TILE, 2 * HDIM), jnp.bfloat16)
        for load in loads:
            load.wait()

        queries = load_queries(0)
        peaks = lax.fori_loop(0, steps_of(0), lambda g, p: score_step(queries, 0, g, p), low)

        def stage_body(stage, row_peaks):
            queries = load_queries(stage)

            def both(g, carry):
                peaks, totals = carry
                totals = value_step(stage - 1, g, row_peaks, totals)
                peaks = score_step(queries, stage, g, peaks)
                return peaks, totals

            peaks, totals = lax.fori_loop(0, steps_of(stage - 1), both, (low, zero))
            finish(stage - 1, totals)
            return to_rows(peaks)

        row_peaks = lax.fori_loop(1, stages, stage_body, to_rows(peaks))
        totals = lax.fori_loop(
            0, steps_of(stages - 1), lambda g, t: value_step(stages - 1, g, row_peaks, t), zero
        )
        finish(stages - 1, totals)


def attend(is_active, tile_slot, tile_mask, qkv):
    rows = qkv.shape[0]
    tiles = rows // TILE
    return pl.pallas_call(
        functools.partial(attend_kernel, is_active),
        out_shape=jax.ShapeDtypeStruct((rows, HDIM), jnp.bfloat16),
        in_specs=[
            pl.BlockSpec(memory_space=pltpu.VMEM),
            pl.BlockSpec(memory_space=pltpu.VMEM),
            pl.BlockSpec(memory_space=pl.ANY),
        ],
        out_specs=pl.BlockSpec(memory_space=pltpu.VMEM),
        scratch_shapes=[
            pltpu.VMEM((rows, 2 * HDIM), jnp.bfloat16),
            pltpu.VMEM((rows + TILE, 2 * HDIM), jnp.bfloat16),
            pltpu.VMEM((2, -(-tiles // GROUP), TOGETHER, TILE, GROUP * TILE), jnp.float32),
            pltpu.VMEM((3, tiles, 128), jnp.int32),
            pltpu.SMEM((3, tiles, 128), jnp.int32),
            pltpu.SemaphoreType.DMA((2,)),
            pltpu.SemaphoreType.DMA,
        ],
        compiler_params=pltpu.CompilerParams(vmem_limit_bytes=60 * 1024 * 1024),
        cost_estimate=pl.CostEstimate(
            flops=4 * rows * rows * HDIM, bytes_accessed=8 * rows * HDIM, transcendentals=rows * rows
        ),
        name="attend",
    )(tile_slot.reshape(1, tiles), tile_mask, qkv)


def sync_peers(peers):
    barrier = pltpu.get_barrier_semaphore()
    for peer in peers:
        pl.semaphore_signal(barrier, inc=1, device_id=peer, device_id_type=MESH)
    pl.semaphore_wait(barrier, len(peers))


def whereabouts(groups, ring):
    ctx, head, part = lax.axis_index("ctx"), lax.axis_index("head"), lax.axis_index("dp")
    shift = lax.rem(part, 2)
    right, left = lax.rem(head + 1, ring), lax.rem(head + ring - 1, ring)
    peers = [(ctx, left, part), (ctx, right, part)]
    peers += [(lax.rem(ctx + i, groups), head, part) for i in range(1, groups)]
    active = lax.rem(ctx + groups - shift, 4) != 3
    return ctx, head, part, shift, right, left, peers, active


def front_kernel(
    groups, ring, heads, patch_ref, wq_ref, wk_ref, wv_ref, out_ref,
    rows_all, weights, stage, weight_sem, own_sem, left_sem, right_sem, pass_sem, far_sem,
    give_sem, self_sem, take_sem,
):
    tokens, width = patch_ref.shape
    chunk = FRONT_ROWS
    chunks = tokens // chunk
    ctx, head, part, shift, right, left, peers, active = whereabouts(groups, ring)
    across = lax.rem(head + 2, ring)

    loads = [
        pltpu.make_async_copy(ref, weights.at[i], weight_sem.at[i])
        for i, ref in enumerate((wq_ref, wk_ref, wv_ref))
    ]
    for load in loads:
        load.start()
    sync_peers(peers)

    def span(c):
        return pl.ds(pl.multiple_of(c * chunk, chunk), chunk)

    def own_copy(c, way, to, sems):
        return pltpu.make_async_remote_copy(
            src_ref=patch_ref.at[span(c), :],
            dst_ref=rows_all.at[head, span(c), :],
            send_sem=own_sem.at[way, c],
            recv_sem=sems.at[c],
            device_id=(ctx, to, part),
            device_id_type=MESH,
        )

    def arrival(slot, c, sems):
        return pltpu.make_async_copy(
            rows_all.at[slot, span(c), :], rows_all.at[slot, span(c), :], sems.at[c]
        )

    def send_own(c):
        own_copy(c, 0, right, left_sem).start()
        own_copy(c, 1, left, right_sem).start()

    def pass_copy(c, slot, to):
        return pltpu.make_async_remote_copy(
            src_ref=rows_all.at[slot, span(c), :],
            dst_ref=rows_all.at[slot, span(c), :],
            send_sem=pass_sem.at[c],
            recv_sem=far_sem.at[c],
            device_id=(ctx, to, part),
            device_id_type=MESH,
        )

    def give_copy(c, i):
        target = lax.rem(ctx + i, groups)
        unit = lax.rem(target + groups - shift, groups)
        owner = jnp.minimum(unit - unit // 4, heads - 1)
        return lax.rem(unit, 4) != 3, pltpu.make_async_remote_copy(
            src_ref=stage.at[owner, span(c), :],
            dst_ref=out_ref.at[ctx, span(c), :],
            send_sem=give_sem.at[i - 1, c],
            recv_sem=take_sem,
            device_id=(target, head, part),
            device_id_type=MESH,
        )

    def keep_copy(c):
        unit = lax.rem(ctx + groups - shift, groups)
        owner = jnp.minimum(unit - unit // 4, heads - 1)
        return pltpu.make_async_copy(
            stage.at[owner, span(c), :], out_ref.at[ctx, span(c), :], self_sem.at[c]
        )

    def project_chunk(c):
        for pair in range(heads // 2):
            cols = slice(pair * 2 * HDIM, (pair + 1) * 2 * HDIM)
            for i in range(3):
                total = jnp.dot(
                    rows_all[0, span(c), :], weights[i, :width, cols],
                    preferred_element_type=jnp.float32,
                )
                for k in range(1, ring):
                    total += jnp.dot(
                        rows_all[k, span(c), :], weights[i, k * width : (k + 1) * width, cols],
                        preferred_element_type=jnp.float32,
                    )
                total = total.astype(jnp.bfloat16)
                for j in range(2):
                    stage[2 * pair + j, span(c), i * HDIM : (i + 1) * HDIM] = total[
                        :, j * HDIM : (j + 1) * HDIM
                    ]
        for i in FRONT_ORDER:
            owned, copy = give_copy(c, i)

            @pl.when(owned)
            def _():
                copy.start()

        @pl.when(active)
        def _():
            keep_copy(c).start()

    ahead = min(FRONT_AHEAD, chunks)
    for c in range(ahead):
        send_own(c)
    rows_all[head] = patch_ref[...]
    for load in loads:
        load.wait()

    def step(c, carry):
        @pl.when(c < chunks)
        def _():
            arrival(left, c, left_sem).wait()
            arrival(right, c, right_sem).wait()

            @pl.when(lax.rem(c, 2) == 0)
            def _():
                pass_copy(c, left, right).start()

            @pl.when(lax.rem(c, 2) == 1)
            def _():
                pass_copy(c, right, left).start()

        @pl.when(c + ahead < chunks)
        def _():
            send_own(c + ahead)

        @pl.when(c >= FRONT_LAG)
        def _():
            arrival(across, c - FRONT_LAG, far_sem).wait()
            project_chunk(c - FRONT_LAG)

        return carry

    lax.fori_loop(0, chunks + FRONT_LAG, step, 0)

    def settle(c, carry):
        own_copy(c, 0, right, left_sem).wait_send()
        own_copy(c, 1, left, right_sem).wait_send()
        pass_copy(c, left, right).wait_send()
        for i in range(1, groups):
            owned, copy = give_copy(c, i)

            @pl.when(owned)
            def _():
                copy.wait_send()

        @pl.when(active)
        def _():
            keep_copy(c).wait()

        return carry

    lax.fori_loop(0, chunks, settle, 0)

    @pl.when(active)
    def _():
        others = pl.ds(0, groups - 1)
        pltpu.make_async_copy(out_ref.at[others], out_ref.at[others], take_sem).wait()


def front(groups, ring, patch_rows, query_weight, key_weight, value_weight):
    tokens, width = patch_rows.shape
    depth, columns = query_weight.shape
    heads = columns // HDIM
    chunks = tokens // FRONT_ROWS
    dma = pltpu.SemaphoreType.DMA
    return pl.pallas_call(
        functools.partial(front_kernel, groups, ring, heads),
        out_shape=jax.ShapeDtypeStruct((groups, tokens, 3 * HDIM), jnp.bfloat16),
        in_specs=[pl.BlockSpec(memory_space=pltpu.VMEM)] + [pl.BlockSpec(memory_space=pl.ANY)] * 3,
        out_specs=pl.BlockSpec(memory_space=pl.ANY),
        scratch_shapes=[
            pltpu.VMEM((ring, tokens, width), jnp.bfloat16),
            pltpu.VMEM((3, depth, columns), jnp.bfloat16),
            pltpu.VMEM((heads, tokens, 3 * HDIM), jnp.bfloat16),
            dma((3,)),
            dma((2, chunks)),
            dma((chunks,)),
            dma((chunks,)),
            dma((chunks,)),
            dma((chunks,)),
            dma((groups - 1, chunks)),
            dma((chunks,)),
            dma,
        ],
        compiler_params=pltpu.CompilerParams(
            collective_id=0, has_side_effects=True, vmem_limit_bytes=60 * 1024 * 1024
        ),
        cost_estimate=pl.CostEstimate(
            flops=6 * tokens * depth * columns, bytes_accessed=8 * depth * columns, transcendentals=0
        ),
        name="front",
    )(patch_rows, query_weight, key_weight, value_weight)


def back_kernel(
    groups, ring, heads, att_ref, wo_ref, out_ref,
    gathered, weights, far_out, far_in, side_out, side_in, own, pending,
    weight_sem, give_sem, self_sem, take_sem, far_send, far_recv, side_send, side_recv,
):
    tokens, width = out_ref.shape
    chunk = BACK_ROWS
    chunks = tokens // chunk
    ctx, head, part, shift, right, left, peers, active = whereabouts(groups, ring)
    across = lax.rem(head + 2, ring)
    unit = lax.rem(ctx + groups - shift, groups)
    mine = jnp.minimum(unit - unit // 4, heads - 1)

    loads = [
        pltpu.make_async_copy(
            wo_ref.at[:, pl.ds(pl.multiple_of(block * width, width), width)],
            weights.at[i],
            weight_sem.at[i],
        )
        for i, block in enumerate((across, right, left, head))
    ]
    for load in loads:
        load.start()
    sync_peers(peers)

    def span(c):
        return pl.ds(pl.multiple_of(c * chunk, chunk), chunk)

    def give_copy(c, i):
        source = lax.rem(ctx + i, groups)
        return pltpu.make_async_remote_copy(
            src_ref=att_ref.at[source, span(c), :],
            dst_ref=gathered.at[mine, span(c), :],
            send_sem=give_sem.at[i - 1, c],
            recv_sem=take_sem.at[c],
            device_id=(source, head, part),
            device_id_type=MESH,
        )

    def keep_copy(c):
        return pltpu.make_async_copy(
            att_ref.at[ctx, span(c), :], gathered.at[mine, span(c), :], self_sem.at[c]
        )

    @pl.when(active)
    def _():
        def give(c, carry):
            keep_copy(c).start()
            for i in range(1, groups):
                give_copy(c, i).start()
            return carry

        lax.fori_loop(0, chunks, give, 0)

    def far_copy(c, to):
        return pltpu.make_async_remote_copy(
            src_ref=far_out.at[span(c), :],
            dst_ref=far_in.at[span(c), :],
            send_sem=far_send.at[c],
            recv_sem=far_recv.at[c],
            device_id=(ctx, to, part),
            device_id_type=MESH,
        )

    def side_copy(c, way, to):
        return pltpu.make_async_remote_copy(
            src_ref=side_out.at[way, span(c), :],
            dst_ref=side_in.at[way, span(c), :],
            send_sem=side_send.at[way, c],
            recv_sem=side_recv.at[way, c],
            device_id=(ctx, to, part),
            device_id_type=MESH,
        )

    for load in loads:
        load.wait()

    def mix(c):
        @pl.when(active)
        def _():
            keep_copy(c).wait()
            others = pl.ds(0, heads - 1)
            pltpu.make_async_copy(
                gathered.at[others, span(c), :], gathered.at[others, span(c), :], take_sem.at[c]
            ).wait()

        @pl.when(jnp.logical_not(active))
        def _():
            pltpu.make_async_copy(
                gathered.at[:, span(c), :], gathered.at[:, span(c), :], take_sem.at[c]
            ).wait()

        rows = jnp.concatenate([gathered[h, span(c), :] for h in range(heads)], axis=1)

        def part_sum(i):
            return jnp.dot(rows, weights[i], preferred_element_type=jnp.float32)

        far_out[span(c), :] = part_sum(0).astype(jnp.bfloat16)
        even = lax.rem(c, 2) == 0

        @pl.when(even)
        def _():
            far_copy(c, right).start()
            side_out[1, span(c), :] = part_sum(2).astype(jnp.bfloat16)
            side_copy(c, 1, left).start()
            pending[span(c), :] = part_sum(1)

        @pl.when(jnp.logical_not(even))
        def _():
            far_copy(c, left).start()
            side_out[0, span(c), :] = part_sum(1).astype(jnp.bfloat16)
            side_copy(c, 0, right).start()
            pending[span(c), :] = part_sum(2)

        own[span(c), :] = part_sum(3)

    def merge(c):
        far_copy(c, right).wait_recv()
        merged = (pending[span(c), :] + far_in[span(c), :].astype(jnp.float32)).astype(jnp.bfloat16)
        even = lax.rem(c, 2) == 0

        @pl.when(even)
        def _():
            side_out[0, span(c), :] = merged
            side_copy(c, 0, right).start()

        @pl.when(jnp.logical_not(even))
        def _():
            side_out[1, span(c), :] = merged
            side_copy(c, 1, left).start()

    def close(c):
        side_copy(c, 0, right).wait_recv()
        side_copy(c, 1, left).wait_recv()
        out_ref[span(c), :] = (
            own[span(c), :]
            + side_in[0, span(c), :].astype(jnp.float32)
            + side_in[1, span(c), :].astype(jnp.float32)
        ).astype(jnp.bfloat16)

    def step(c, carry):
        @pl.when((c >= BACK_LAG) & (c < chunks + BACK_LAG))
        def _():
            merge(c - BACK_LAG)

        @pl.when(c < chunks)
        def _():
            mix(c)

        @pl.when(c >= 2 * BACK_LAG)
        def _():
            close(c - 2 * BACK_LAG)

        return carry

    lax.fori_loop(0, chunks + 2 * BACK_LAG, step, 0)

    def settle(c, carry):
        far_copy(c, right).wait_send()
        side_copy(c, 0, right).wait_send()
        side_copy(c, 1, left).wait_send()

        @pl.when(active)
        def _():
            for i in range(1, groups):
                give_copy(c, i).wait_send()

        return carry

    lax.fori_loop(0, chunks, settle, 0)


def back(groups, ring, attended, output_weight):
    tokens = attended.shape[1]
    columns, depth = output_weight.shape
    width = depth // ring
    heads = columns // HDIM
    chunks = tokens // BACK_ROWS
    dma = pltpu.SemaphoreType.DMA
    return pl.pallas_call(
        functools.partial(back_kernel, groups, ring, heads),
        out_shape=jax.ShapeDtypeStruct((tokens, width), jnp.bfloat16),
        in_specs=[pl.BlockSpec(memory_space=pl.ANY)] * 2,
        out_specs=pl.BlockSpec(memory_space=pltpu.VMEM),
        scratch_shapes=[
            pltpu.VMEM((heads, tokens, HDIM), jnp.bfloat16),
            pltpu.VMEM((ring, columns, width), jnp.bfloat16),
            pltpu.VMEM((tokens, width), jnp.bfloat16),
            pltpu.VMEM((tokens, width), jnp.bfloat16),
            pltpu.VMEM((2, tokens, width), jnp.bfloat16),
            pltpu.VMEM((2, tokens, width), jnp.bfloat16),
            pltpu.VMEM((tokens, width), jnp.float32),
            pltpu.VMEM((tokens, width), jnp.float32),
            dma((ring,)),
            dma((groups - 1, chunks)),
            dma((chunks,)),
            dma((chunks,)),
            dma((chunks,)),
            dma((chunks,)),
            dma((2, chunks)),
            dma((2, chunks)),
        ],
        compiler_params=pltpu.CompilerParams(
            collective_id=1, has_side_effects=True, vmem_limit_bytes=60 * 1024 * 1024
        ),
        cost_estimate=pl.CostEstimate(
            flops=2 * tokens * depth * columns, bytes_accessed=2 * depth * columns, transcendentals=0
        ),
        name="back",
    )(attended, output_weight)


def body(patch_rows, query_weight, key_weight, value_weight, output_weight, tile_slot, tile_mask):
    groups = lax.axis_size("ctx")
    tokens = patch_rows.shape[0]
    ring = lax.axis_size("head")
    sent = front(groups, ring, patch_rows, query_weight, key_weight, value_weight)

    def is_active():
        return whereabouts(groups, ring)[-1]

    attended = attend(is_active, tile_slot, tile_mask, sent.reshape(groups * tokens, 3 * HDIM))
    return back(groups, ring, attended.reshape(groups, tokens, HDIM), output_weight)


def solution(mesh):
    in_specs = (
        P(("dp", "ctx"), "head"),
        P(None, "head"),
        P(None, "head"),
        P(None, "head"),
        P("head", None),
        P("dp"),
        P("dp", None),
    )
    out_specs = P(("dp", "ctx"), "head")
    return jax.shard_map(body, mesh=mesh, in_specs=in_specs, out_specs=out_specs, check_vma=False)
```

```python
import functools
import math

import jax
import jax.numpy as jnp
from jax import lax
from jax.experimental import pallas as pl
from jax.experimental.pallas import tpu as pltpu
from jax.sharding import PartitionSpec as P

HDIM = 128
TILE = 128
GROUP = 12
TOGETHER = 3
WIDE = 6
FRONT_ROWS = 64
FRONT_AHEAD = 2
FRONT_LAG = 1
FRONT_ORDER = (1, 2, 3, 4, 5, 6, 7)
BACK_ROWS = 128
BACK_LAG = 2
MESH = pl.DeviceIdType.MESH
LOG2E = 1.4426950408889634


def attend_kernel(
    is_active, slot_ref, mask_ref, qkv_ref, out_ref,
    query_key, values, scores, plan_rows, plan, load_sem, plan_sem,
):
    tokens = out_ref.shape[0]
    tiles = tokens // TILE
    stages = tiles // TOGETHER
    factor = LOG2E / math.sqrt(HDIM)

    def at(tile):
        return pl.ds(pl.multiple_of(tile * TILE, TILE), TILE)

    def make_plan():
        def iota(shape, axis):
            return lax.broadcasted_iota(jnp.int32, shape, axis)

        def product(a, b, dims=((1,), (0,))):
            return lax.dot_general(a, b, (dims, ((), ())), preferred_element_type=jnp.float32)

        square = (tiles, tiles)
        row, col = iota(square, 0), iota(square, 1)
        home = (slot_ref[...] == row).astype(jnp.float32)
        mask = (mask_ref[...] == 1).astype(jnp.float32)
        size = jnp.sum(mask, axis=1, keepdims=True)
        size_row = product(jnp.ones((1, tiles), jnp.float32), mask, ((1,), (1,)))
        ahead = (size > size_row) | ((size == size_row) & (row < col))
        position = jnp.sum(ahead.astype(jnp.float32), axis=0, keepdims=True)
        arrange = (position == row.astype(jnp.float32)).astype(jnp.float32)
        chosen = product(arrange, home)
        order = jnp.sum(chosen * col.astype(jnp.float32), axis=1, keepdims=True)
        live = product(product(arrange, mask), home)
        rank = product(live, (row <= col).astype(jnp.float32))
        count = jnp.sum(live, axis=1, keepdims=True)
        rank = jnp.where(live > 0.5, rank - 1.0, -1.0)
        lane = iota((tiles, 128), 1).astype(jnp.float32)
        listed = jnp.zeros((tiles, 128), jnp.float32)
        for u in range(1, tiles):
            listed += jnp.where(rank[:, u : u + 1] == lane, float(u), 0.0)
        used = lane < count
        plan_rows[0] = jnp.where(used, listed, listed[:, :1]).astype(jnp.int32)
        plan_rows[1] = jnp.where(used, listed, float(tiles)).astype(jnp.int32)
        plan_rows[2] = jnp.where(lane == 0.0, order, count).astype(jnp.int32)
        move = pltpu.make_async_copy(plan_rows, plan, plan_sem)
        move.start()
        move.wait()

    def score_step(queries, stage, g, peaks, size=GROUP):
        fresh = []
        for j in range(TOGETHER):
            r, base = stage * TOGETHER + j, g * GROUP
            peak = peaks[j]
            for i in range(0, size, WIDE):
                block = jnp.concatenate(
                    [query_key[at(plan[0, r, base + i + k]), HDIM:] for k in range(WIDE)], axis=0
                )
                found = lax.dot_general(
                    queries[j], block, (((1,), (1,)), ((), ())), preferred_element_type=jnp.float32
                )
                scores[lax.rem(stage, 2), g, j, :, i * TILE : (i + WIDE) * TILE] = found
                for k in range(WIDE):
                    peak = jnp.maximum(peak, found[:, k * TILE : (k + 1) * TILE])
            fresh.append(peak)
        return tuple(fresh)

    def value_step(stage, g, row_peaks, totals, size=GROUP):
        fresh = []
        for j in range(TOGETHER):
            r, base = stage * TOGETHER + j, g * GROUP
            weight = jnp.exp2(
                scores[lax.rem(stage, 2), g, j, :, : size * TILE] * factor - row_peaks[j]
            ).astype(jnp.bfloat16)
            block = jnp.concatenate([values[at(plan[1, r, base + i]), :] for i in range(size)], axis=0)
            fresh.append(totals[j] + jnp.dot(weight, block, preferred_element_type=jnp.float32))
        return tuple(fresh)

    def tile_of(stage, j):
        return plan[2, stage * TOGETHER + j, 0]

    def load_queries(stage):
        return [query_key[at(tile_of(stage, j)), :HDIM] for j in range(TOGETHER)]

    def over_steps(stage, step, carry):
        half = GROUP // 2
        halves = (plan[2, stage * TOGETHER, 1] + half - 1) // half
        whole = halves // 2
        carry = lax.fori_loop(0, whole, lambda g, c: step(g, c, GROUP), carry)
        return lax.fori_loop(whole, halves - whole, lambda g, c: step(g, c, half), carry)

    def to_rows(peaks):
        return tuple(jnp.max(peak, axis=1, keepdims=True) * factor for peak in peaks)

    def finish(stage, totals):
        for j in range(TOGETHER):
            out_ref[at(tile_of(stage, j)), :] = (
                totals[j][:, :HDIM] / totals[j][:, HDIM:]
            ).astype(jnp.bfloat16)

    low = tuple(jnp.full((TILE, TILE), -jnp.inf, jnp.float32) for _ in range(TOGETHER))
    zero = tuple(jnp.zeros((TILE, 2 * HDIM), jnp.float32) for _ in range(TOGETHER))

    @pl.when(is_active())
    def _():
        loads = [
            pltpu.make_async_copy(qkv_ref.at[:, : 2 * HDIM], query_key, load_sem.at[0]),
            pltpu.make_async_copy(
                qkv_ref.at[:, 2 * HDIM :], values.at[pl.ds(0, tokens), pl.ds(0, HDIM)], load_sem.at[1]
            ),
        ]
        for load in loads:
            load.start()
        make_plan()
        values[pl.ds(0, tokens), HDIM:] = jnp.ones((tokens, HDIM), jnp.bfloat16)
        values[pl.ds(tokens, TILE), :] = jnp.zeros((TILE, 2 * HDIM), jnp.bfloat16)
        for load in loads:
            load.wait()

        queries = load_queries(0)
        peaks = over_steps(0, lambda g, p, size: score_step(queries, 0, g, p, size), low)

        def stage_body(stage, row_peaks):
            queries = load_queries(stage)

            def both(g, carry, size):
                peaks, totals = carry
                totals = value_step(stage - 1, g, row_peaks, totals, size)
                peaks = score_step(queries, stage, g, peaks, size)
                return peaks, totals

            peaks, totals = over_steps(stage - 1, both, (low, zero))
            finish(stage - 1, totals)
            return to_rows(peaks)

        row_peaks = lax.fori_loop(1, stages, stage_body, to_rows(peaks))
        totals = over_steps(
            stages - 1, lambda g, t, size: value_step(stages - 1, g, row_peaks, t, size), zero
        )
        finish(stages - 1, totals)


def attend(is_active, tile_slot, tile_mask, qkv):
    rows = qkv.shape[0]
    tiles = rows // TILE
    return pl.pallas_call(
        functools.partial(attend_kernel, is_active),
        out_shape=jax.ShapeDtypeStruct((rows, HDIM), jnp.bfloat16),
        in_specs=[
            pl.BlockSpec(memory_space=pltpu.VMEM),
            pl.BlockSpec(memory_space=pltpu.VMEM),
            pl.BlockSpec(memory_space=pl.ANY),
        ],
        out_specs=pl.BlockSpec(memory_space=pltpu.VMEM),
        scratch_shapes=[
            pltpu.VMEM((rows, 2 * HDIM), jnp.bfloat16),
            pltpu.VMEM((rows + TILE, 2 * HDIM), jnp.bfloat16),
            pltpu.VMEM((2, -(-tiles // GROUP), TOGETHER, TILE, GROUP * TILE), jnp.float32),
            pltpu.VMEM((3, tiles, 128), jnp.int32),
            pltpu.SMEM((3, tiles, 128), jnp.int32),
            pltpu.SemaphoreType.DMA((2,)),
            pltpu.SemaphoreType.DMA,
        ],
        compiler_params=pltpu.CompilerParams(vmem_limit_bytes=56 * 1024 * 1024),
        cost_estimate=pl.CostEstimate(
            flops=4 * rows * rows * HDIM, bytes_accessed=8 * rows * HDIM, transcendentals=rows * rows
        ),
        name="attend",
    )(tile_slot.reshape(1, tiles), tile_mask, qkv)


def sync_peers(peers):
    barrier = pltpu.get_barrier_semaphore()
    for peer in peers:
        pl.semaphore_signal(barrier, inc=1, device_id=peer, device_id_type=MESH)
    pl.semaphore_wait(barrier, len(peers))


def whereabouts(groups, ring):
    ctx, head, part = lax.axis_index("ctx"), lax.axis_index("head"), lax.axis_index("dp")
    shift = lax.rem(part, 2)
    right, left = lax.rem(head + 1, ring), lax.rem(head + ring - 1, ring)
    peers = [(ctx, left, part), (ctx, right, part)]
    peers += [(lax.rem(ctx + i, groups), head, part) for i in range(1, groups)]
    active = lax.rem(ctx + groups - shift, 4) != 3
    return ctx, head, part, shift, right, left, peers, active


def front_kernel(
    groups, ring, heads, patch_ref, wq_ref, wk_ref, wv_ref, out_ref,
    rows_all, weights, stage, weight_sem, own_sem, left_sem, right_sem, pass_sem, far_sem,
    give_sem, self_sem, take_sem,
):
    tokens, width = patch_ref.shape
    chunk = FRONT_ROWS
    chunks = tokens // chunk
    ctx, head, part, shift, right, left, peers, active = whereabouts(groups, ring)
    across = lax.rem(head + 2, ring)

    loads = [
        pltpu.make_async_copy(ref, weights.at[i], weight_sem.at[i])
        for i, ref in enumerate((wq_ref, wk_ref, wv_ref))
    ]
    for load in loads:
        load.start()
    sync_peers(peers)

    def span(c):
        return pl.ds(pl.multiple_of(c * chunk, chunk), chunk)

    def own_copy(c, way, to, sems):
        return pltpu.make_async_remote_copy(
            src_ref=patch_ref.at[span(c), :],
            dst_ref=rows_all.at[head, span(c), :],
            send_sem=own_sem.at[way, c],
            recv_sem=sems.at[c],
            device_id=(ctx, to, part),
            device_id_type=MESH,
        )

    def arrival(slot, c, sems):
        return pltpu.make_async_copy(
            rows_all.at[slot, span(c), :], rows_all.at[slot, span(c), :], sems.at[c]
        )

    def send_own(c):
        own_copy(c, 0, right, left_sem).start()
        own_copy(c, 1, left, right_sem).start()

    def half(c, i):
        return pl.ds(pl.multiple_of(c * chunk + i * (chunk // 2), chunk // 2), chunk // 2)

    def pass_copy(c, i):
        slot, to = ((left, right), (right, left))[i]
        return pltpu.make_async_remote_copy(
            src_ref=rows_all.at[slot, half(c, i), :],
            dst_ref=rows_all.at[slot, half(c, i), :],
            send_sem=pass_sem.at[i, c],
            recv_sem=far_sem.at[i, c],
            device_id=(ctx, to, part),
            device_id_type=MESH,
        )

    def far_arrival(c, i):
        return pltpu.make_async_copy(
            rows_all.at[across, half(c, i), :], rows_all.at[across, half(c, i), :], far_sem.at[i, c]
        )

    def give_copy(c, i):
        target = lax.rem(ctx + i, groups)
        unit = lax.rem(target + groups - shift, groups)
        owner = jnp.minimum(unit - unit // 4, heads - 1)
        return lax.rem(unit, 4) != 3, pltpu.make_async_remote_copy(
            src_ref=stage.at[owner, span(c), :],
            dst_ref=out_ref.at[ctx, span(c), :],
            send_sem=give_sem.at[i - 1, c],
            recv_sem=take_sem,
            device_id=(target, head, part),
            device_id_type=MESH,
        )

    def keep_copy(c):
        unit = lax.rem(ctx + groups - shift, groups)
        owner = jnp.minimum(unit - unit // 4, heads - 1)
        return pltpu.make_async_copy(
            stage.at[owner, span(c), :], out_ref.at[ctx, span(c), :], self_sem.at[c]
        )

    def project_chunk(c):
        for pair in range(heads // 2):
            cols = slice(pair * 2 * HDIM, (pair + 1) * 2 * HDIM)
            for i in range(3):
                total = jnp.dot(
                    rows_all[0, span(c), :], weights[i, :width, cols],
                    preferred_element_type=jnp.float32,
                )
                for k in range(1, ring):
                    total += jnp.dot(
                        rows_all[k, span(c), :], weights[i, k * width : (k + 1) * width, cols],
                        preferred_element_type=jnp.float32,
                    )
                total = total.astype(jnp.bfloat16)
                for j in range(2):
                    stage[2 * pair + j, span(c), i * HDIM : (i + 1) * HDIM] = total[
                        :, j * HDIM : (j + 1) * HDIM
                    ]
        for i in FRONT_ORDER:
            owned, copy = give_copy(c, i)

            @pl.when(owned)
            def _():
                copy.start()

        @pl.when(active)
        def _():
            keep_copy(c).start()

    ahead = min(FRONT_AHEAD, chunks)
    for c in range(ahead):
        send_own(c)
    rows_all[head] = patch_ref[...]

    def step(c, carry):
        @pl.when(c < chunks)
        def _():
            arrival(left, c, left_sem).wait()
            pass_copy(c, 0).start()
            arrival(right, c, right_sem).wait()
            pass_copy(c, 1).start()

        @pl.when(c + ahead < chunks)
        def _():
            send_own(c + ahead)

        @pl.when(c >= FRONT_LAG)
        def _():
            for i in range(2):
                far_arrival(c - FRONT_LAG, i).wait()

            @pl.when(c == FRONT_LAG)
            def _():
                for load in loads:
                    load.wait()

            project_chunk(c - FRONT_LAG)

        return carry

    lax.fori_loop(0, chunks + FRONT_LAG, step, 0)

    def settle(c, carry):
        own_copy(c, 0, right, left_sem).wait_send()
        own_copy(c, 1, left, right_sem).wait_send()
        pass_copy(c, 0).wait_send()
        pass_copy(c, 1).wait_send()
        for i in range(1, groups):
            owned, copy = give_copy(c, i)

            @pl.when(owned)
            def _():
                copy.wait_send()

        @pl.when(active)
        def _():
            keep_copy(c).wait()

        return carry

    lax.fori_loop(0, chunks, settle, 0)

    @pl.when(active)
    def _():
        others = pl.ds(0, groups - 1)
        pltpu.make_async_copy(out_ref.at[others], out_ref.at[others], take_sem).wait()


def front(groups, ring, patch_rows, query_weight, key_weight, value_weight):
    tokens, width = patch_rows.shape
    depth, columns = query_weight.shape
    heads = columns // HDIM
    chunks = tokens // FRONT_ROWS
    dma = pltpu.SemaphoreType.DMA
    return pl.pallas_call(
        functools.partial(front_kernel, groups, ring, heads),
        out_shape=jax.ShapeDtypeStruct((groups, tokens, 3 * HDIM), jnp.bfloat16),
        in_specs=[pl.BlockSpec(memory_space=pltpu.VMEM)] + [pl.BlockSpec(memory_space=pl.ANY)] * 3,
        out_specs=pl.BlockSpec(memory_space=pl.ANY),
        scratch_shapes=[
            pltpu.VMEM((ring, tokens, width), jnp.bfloat16),
            pltpu.VMEM((3, depth, columns), jnp.bfloat16),
            pltpu.VMEM((heads, tokens, 3 * HDIM), jnp.bfloat16),
            dma((3,)),
            dma((2, chunks)),
            dma((chunks,)),
            dma((chunks,)),
            dma((2, chunks)),
            dma((2, chunks)),
            dma((groups - 1, chunks)),
            dma((chunks,)),
            dma,
        ],
        compiler_params=pltpu.CompilerParams(
            collective_id=0, has_side_effects=True, vmem_limit_bytes=60 * 1024 * 1024
        ),
        cost_estimate=pl.CostEstimate(
            flops=6 * tokens * depth * columns, bytes_accessed=8 * depth * columns, transcendentals=0
        ),
        name="front",
    )(patch_rows, query_weight, key_weight, value_weight)


def back_kernel(
    groups, ring, heads, att_ref, wo_ref, out_ref,
    gathered, weights, far_out, far_in, side_out, side_in, own, pending,
    weight_sem, give_sem, self_sem, take_sem, far_send, far_recv, side_send, side_recv,
):
    tokens, width = out_ref.shape
    chunk = BACK_ROWS
    chunks = tokens // chunk
    ctx, head, part, shift, right, left, peers, active = whereabouts(groups, ring)
    across = lax.rem(head + 2, ring)
    unit = lax.rem(ctx + groups - shift, groups)
    mine = jnp.minimum(unit - unit // 4, heads - 1)

    loads = [
        pltpu.make_async_copy(
            wo_ref.at[:, pl.ds(pl.multiple_of(block * width, width), width)],
            weights.at[i],
            weight_sem.at[i],
        )
        for i, block in enumerate((across, right, left, head))
    ]
    for load in loads:
        load.start()
    sync_peers(peers)

    def span(c):
        return pl.ds(pl.multiple_of(c * chunk, chunk), chunk)

    def give_copy(c, i):
        source = lax.rem(ctx + i, groups)
        return pltpu.make_async_remote_copy(
            src_ref=att_ref.at[source, span(c), :],
            dst_ref=gathered.at[mine, span(c), :],
            send_sem=give_sem.at[i - 1, c],
            recv_sem=take_sem.at[c],
            device_id=(source, head, part),
            device_id_type=MESH,
        )

    def keep_copy(c):
        return pltpu.make_async_copy(
            att_ref.at[ctx, span(c), :], gathered.at[mine, span(c), :], self_sem.at[c]
        )

    @pl.when(active)
    def _():
        def give(c, carry):
            keep_copy(c).start()
            for i in range(1, groups):
                give_copy(c, i).start()
            return carry

        lax.fori_loop(0, chunks, give, 0)

    def half(c, i):
        return pl.ds(pl.multiple_of(c * chunk + i * (chunk // 2), chunk // 2), chunk // 2)

    def far_copy(c, i):
        return pltpu.make_async_remote_copy(
            src_ref=far_out.at[half(c, i), :],
            dst_ref=far_in.at[half(c, i), :],
            send_sem=far_send.at[i, c],
            recv_sem=far_recv.at[i, c],
            device_id=(ctx, (right, left)[i], part),
            device_id_type=MESH,
        )

    def side_copy(c, way, i):
        return pltpu.make_async_remote_copy(
            src_ref=side_out.at[way, half(c, i), :],
            dst_ref=side_in.at[way, half(c, i), :],
            send_sem=side_send.at[2 * way + i, c],
            recv_sem=side_recv.at[2 * way + i, c],
            device_id=(ctx, (right, left)[way], part),
            device_id_type=MESH,
        )

    for load in loads:
        load.wait()

    def mix(c):
        @pl.when(active)
        def _():
            keep_copy(c).wait()
            others = pl.ds(0, heads - 1)
            pltpu.make_async_copy(
                gathered.at[others, span(c), :], gathered.at[others, span(c), :], take_sem.at[c]
            ).wait()

        @pl.when(jnp.logical_not(active))
        def _():
            pltpu.make_async_copy(
                gathered.at[:, span(c), :], gathered.at[:, span(c), :], take_sem.at[c]
            ).wait()

        rows = jnp.concatenate([gathered[h, span(c), :] for h in range(heads)], axis=1)

        def part_sum(i):
            return jnp.dot(rows, weights[i], preferred_element_type=jnp.float32)

        far_out[span(c), :] = part_sum(0).astype(jnp.bfloat16)
        far_copy(c, 0).start()
        far_copy(c, 1).start()
        middle = chunk // 2
        to_right, to_left = part_sum(1), part_sum(2)
        side_out[0, half(c, 1), :] = to_right[middle:].astype(jnp.bfloat16)
        side_copy(c, 0, 1).start()
        side_out[1, half(c, 0), :] = to_left[:middle].astype(jnp.bfloat16)
        side_copy(c, 1, 0).start()
        pending[half(c, 0), :] = to_right[:middle]
        pending[half(c, 1), :] = to_left[middle:]
        own[span(c), :] = part_sum(3)

    def merge(c):
        for i in range(2):
            far_copy(c, i).wait_recv()
            side_out[i, half(c, i), :] = (
                pending[half(c, i), :] + far_in[half(c, i), :].astype(jnp.float32)
            ).astype(jnp.bfloat16)
            side_copy(c, i, i).start()

    def close(c):
        for way in range(2):
            for i in range(2):
                side_copy(c, way, i).wait_recv()
        out_ref[span(c), :] = (
            own[span(c), :]
            + side_in[0, span(c), :].astype(jnp.float32)
            + side_in[1, span(c), :].astype(jnp.float32)
        ).astype(jnp.bfloat16)

    def step(c, carry):
        @pl.when((c >= BACK_LAG) & (c < chunks + BACK_LAG))
        def _():
            merge(c - BACK_LAG)

        @pl.when(c < chunks)
        def _():
            mix(c)

        @pl.when(c >= 2 * BACK_LAG)
        def _():
            close(c - 2 * BACK_LAG)

        return carry

    lax.fori_loop(0, chunks + 2 * BACK_LAG, step, 0)

    def settle(c, carry):
        for i in range(2):
            far_copy(c, i).wait_send()
            side_copy(c, 0, i).wait_send()
            side_copy(c, 1, i).wait_send()

        @pl.when(active)
        def _():
            for i in range(1, groups):
                give_copy(c, i).wait_send()

        return carry

    lax.fori_loop(0, chunks, settle, 0)


def back(groups, ring, attended, output_weight):
    tokens = attended.shape[1]
    columns, depth = output_weight.shape
    width = depth // ring
    heads = columns // HDIM
    chunks = tokens // BACK_ROWS
    dma = pltpu.SemaphoreType.DMA
    return pl.pallas_call(
        functools.partial(back_kernel, groups, ring, heads),
        out_shape=jax.ShapeDtypeStruct((tokens, width), jnp.bfloat16),
        in_specs=[pl.BlockSpec(memory_space=pl.ANY)] * 2,
        out_specs=pl.BlockSpec(memory_space=pltpu.VMEM),
        scratch_shapes=[
            pltpu.VMEM((heads, tokens, HDIM), jnp.bfloat16),
            pltpu.VMEM((ring, columns, width), jnp.bfloat16),
            pltpu.VMEM((tokens, width), jnp.bfloat16),
            pltpu.VMEM((tokens, width), jnp.bfloat16),
            pltpu.VMEM((2, tokens, width), jnp.bfloat16),
            pltpu.VMEM((2, tokens, width), jnp.bfloat16),
            pltpu.VMEM((tokens, width), jnp.float32),
            pltpu.VMEM((tokens, width), jnp.float32),
            dma((ring,)),
            dma((groups - 1, chunks)),
            dma((chunks,)),
            dma((chunks,)),
            dma((2, chunks)),
            dma((2, chunks)),
            dma((4, chunks)),
            dma((4, chunks)),
        ],
        compiler_params=pltpu.CompilerParams(
            collective_id=1, has_side_effects=True, vmem_limit_bytes=60 * 1024 * 1024
        ),
        cost_estimate=pl.CostEstimate(
            flops=2 * tokens * depth * columns, bytes_accessed=2 * depth * columns, transcendentals=0
        ),
        name="back",
    )(attended, output_weight)


def body(patch_rows, query_weight, key_weight, value_weight, output_weight, tile_slot, tile_mask):
    groups = lax.axis_size("ctx")
    tokens = patch_rows.shape[0]
    ring = lax.axis_size("head")
    sent = front(groups, ring, patch_rows, query_weight, key_weight, value_weight)

    def is_active():
        return whereabouts(groups, ring)[-1]

    attended = attend(is_active, tile_slot, tile_mask, sent.reshape(groups * tokens, 3 * HDIM))
    return back(groups, ring, attended.reshape(groups, tokens, HDIM), output_weight)


def solution(mesh):
    in_specs = (
        P(("dp", "ctx"), "head"),
        P(None, "head"),
        P(None, "head"),
        P(None, "head"),
        P("head", None),
        P("dp"),
        P("dp", None),
    )
    out_specs = P(("dp", "ctx"), "head")
    return jax.shard_map(body, mesh=mesh, in_specs=in_specs, out_specs=out_specs, check_vma=False)
```

```python
import functools
import math

import jax
import jax.numpy as jnp
from jax import lax
from jax.experimental import pallas as pl
from jax.experimental.pallas import tpu as pltpu
from jax.sharding import PartitionSpec as P

HDIM = 128
TILE = 128
GROUP = 12
TOGETHER = 3
WIDE = 6
FRONT_ROWS = 64
FRONT_AHEAD = 2
FRONT_LAG = 1
FRONT_ORDER = (1, 2, 3, 4, 5, 6, 7)
BACK_ROWS = 128
BACK_LAG = 2
MESH = pl.DeviceIdType.MESH
LOG2E = 1.4426950408889634


def attend_kernel(
    is_active, slot_ref, mask_ref, qkv_ref, out_ref,
    query_key, values, scores, plan_rows, plan, load_sem, plan_sem,
):
    tokens = out_ref.shape[0]
    tiles = tokens // TILE
    stages = tiles // TOGETHER
    factor = LOG2E / math.sqrt(HDIM)

    def at(tile):
        return pl.ds(pl.multiple_of(tile * TILE, TILE), TILE)

    def make_plan():
        def iota(shape, axis):
            return lax.broadcasted_iota(jnp.int32, shape, axis)

        def product(a, b, dims=((1,), (0,))):
            return lax.dot_general(a, b, (dims, ((), ())), preferred_element_type=jnp.float32)

        square = (tiles, tiles)
        row, col = iota(square, 0), iota(square, 1)
        home = (slot_ref[...] == row).astype(jnp.float32)
        mask = (mask_ref[...] == 1).astype(jnp.float32)
        size = jnp.sum(mask, axis=1, keepdims=True)
        size_row = product(jnp.ones((1, tiles), jnp.float32), mask, ((1,), (1,)))
        ahead = (size > size_row) | ((size == size_row) & (row < col))
        position = jnp.sum(ahead.astype(jnp.float32), axis=0, keepdims=True)
        arrange = (position == row.astype(jnp.float32)).astype(jnp.float32)
        chosen = product(arrange, home)
        order = jnp.sum(chosen * col.astype(jnp.float32), axis=1, keepdims=True)
        live = product(product(arrange, mask), home)
        rank = product(live, (row <= col).astype(jnp.float32))
        count = jnp.sum(live, axis=1, keepdims=True)
        rank = jnp.where(live > 0.5, rank - 1.0, -1.0)
        lane = iota((tiles, 128), 1).astype(jnp.float32)
        listed = jnp.zeros((tiles, 128), jnp.float32)
        for u in range(1, tiles):
            listed += jnp.where(rank[:, u : u + 1] == lane, float(u), 0.0)
        used = lane < count
        plan_rows[0] = jnp.where(used, listed, listed[:, :1]).astype(jnp.int32)
        plan_rows[1] = jnp.where(used, listed, float(tiles)).astype(jnp.int32)
        plan_rows[2] = jnp.where(lane == 0.0, order, count).astype(jnp.int32)
        move = pltpu.make_async_copy(plan_rows, plan, plan_sem)
        move.start()
        move.wait()

    def score_step(queries, stage, g, peaks, size=GROUP):
        fresh = []
        for j in range(TOGETHER):
            r, base = stage * TOGETHER + j, g * GROUP
            peak = peaks[j]
            for i in range(0, size, WIDE):
                block = jnp.concatenate(
                    [query_key[at(plan[0, r, base + i + k]), HDIM:] for k in range(WIDE)], axis=0
                )
                found = lax.dot_general(
                    queries[j], block, (((1,), (1,)), ((), ())), preferred_element_type=jnp.float32
                )
                scores[lax.rem(stage, 2), g, j, :, i * TILE : (i + WIDE) * TILE] = found
                for k in range(WIDE):
                    peak = jnp.maximum(peak, found[:, k * TILE : (k + 1) * TILE])
            fresh.append(peak)
        return tuple(fresh)

    def value_step(stage, g, row_peaks, totals, size=GROUP):
        fresh = []
        for j in range(TOGETHER):
            r, base = stage * TOGETHER + j, g * GROUP
            weight = jnp.exp2(
                scores[lax.rem(stage, 2), g, j, :, : size * TILE] * factor - row_peaks[j]
            ).astype(jnp.bfloat16)
            block = jnp.concatenate([values[at(plan[1, r, base + i]), :] for i in range(size)], axis=0)
            fresh.append(totals[j] + jnp.dot(weight, block, preferred_element_type=jnp.float32))
        return tuple(fresh)

    def tile_of(stage, j):
        return plan[2, stage * TOGETHER + j, 0]

    def load_queries(stage):
        return [query_key[at(tile_of(stage, j)), :HDIM] for j in range(TOGETHER)]

    def over_steps(stage, step, carry):
        half = GROUP // 2
        halves = (plan[2, stage * TOGETHER, 1] + half - 1) // half
        whole = halves // 2
        carry = lax.fori_loop(0, whole, lambda g, c: step(g, c, GROUP), carry)
        return lax.fori_loop(whole, halves - whole, lambda g, c: step(g, c, half), carry)

    def to_rows(peaks):
        return tuple(jnp.max(peak, axis=1, keepdims=True) * factor for peak in peaks)

    def finish(stage, totals):
        for j in range(TOGETHER):
            out_ref[at(tile_of(stage, j)), :] = (
                totals[j][:, :HDIM] / totals[j][:, HDIM:]
            ).astype(jnp.bfloat16)

    low = tuple(jnp.full((TILE, TILE), -jnp.inf, jnp.float32) for _ in range(TOGETHER))
    zero = tuple(jnp.zeros((TILE, 2 * HDIM), jnp.float32) for _ in range(TOGETHER))

    @pl.when(is_active())
    def _():
        loads = [
            pltpu.make_async_copy(qkv_ref.at[:, : 2 * HDIM], query_key, load_sem.at[0]),
            pltpu.make_async_copy(
                qkv_ref.at[:, 2 * HDIM :], values.at[pl.ds(0, tokens), pl.ds(0, HDIM)], load_sem.at[1]
            ),
        ]
        for load in loads:
            load.start()
        make_plan()
        values[pl.ds(0, tokens), HDIM:] = jnp.ones((tokens, HDIM), jnp.bfloat16)
        values[pl.ds(tokens, TILE), :] = jnp.zeros((TILE, 2 * HDIM), jnp.bfloat16)
        for load in loads:
            load.wait()

        queries = load_queries(0)
        peaks = over_steps(0, lambda g, p, size: score_step(queries, 0, g, p, size), low)

        def stage_body(stage, row_peaks):
            queries = load_queries(stage)

            def both(g, carry, size):
                peaks, totals = carry
                totals = value_step(stage - 1, g, row_peaks, totals, size)
                peaks = score_step(queries, stage, g, peaks, size)
                return peaks, totals

            peaks, totals = over_steps(stage - 1, both, (low, zero))
            finish(stage - 1, totals)
            return to_rows(peaks)

        row_peaks = lax.fori_loop(1, stages, stage_body, to_rows(peaks))
        totals = over_steps(
            stages - 1, lambda g, t, size: value_step(stages - 1, g, row_peaks, t, size), zero
        )
        finish(stages - 1, totals)


def attend(is_active, tile_slot, tile_mask, qkv):
    rows = qkv.shape[0]
    tiles = rows // TILE
    return pl.pallas_call(
        functools.partial(attend_kernel, is_active),
        out_shape=jax.ShapeDtypeStruct((rows, HDIM), jnp.bfloat16),
        in_specs=[
            pl.BlockSpec(memory_space=pltpu.VMEM),
            pl.BlockSpec(memory_space=pltpu.VMEM),
            pl.BlockSpec(memory_space=pl.ANY),
        ],
        out_specs=pl.BlockSpec(memory_space=pltpu.VMEM),
        scratch_shapes=[
            pltpu.VMEM((rows, 2 * HDIM), jnp.bfloat16),
            pltpu.VMEM((rows + TILE, 2 * HDIM), jnp.bfloat16),
            pltpu.VMEM((2, -(-tiles // GROUP), TOGETHER, TILE, GROUP * TILE), jnp.float32),
            pltpu.VMEM((3, tiles, 128), jnp.int32),
            pltpu.SMEM((3, tiles, 128), jnp.int32),
            pltpu.SemaphoreType.DMA((2,)),
            pltpu.SemaphoreType.DMA,
        ],
        compiler_params=pltpu.CompilerParams(vmem_limit_bytes=56 * 1024 * 1024),
        cost_estimate=pl.CostEstimate(
            flops=4 * rows * rows * HDIM, bytes_accessed=8 * rows * HDIM, transcendentals=rows * rows
        ),
        name="attend",
    )(tile_slot.reshape(1, tiles), tile_mask, qkv)


def sync_peers(peers):
    barrier = pltpu.get_barrier_semaphore()
    for peer in peers:
        pl.semaphore_signal(barrier, inc=1, device_id=peer, device_id_type=MESH)
    pl.semaphore_wait(barrier, len(peers))


def whereabouts(groups, ring):
    ctx, head, part = lax.axis_index("ctx"), lax.axis_index("head"), lax.axis_index("dp")
    shift = lax.rem(part, 2)
    right, left = lax.rem(head + 1, ring), lax.rem(head + ring - 1, ring)
    peers = [(ctx, left, part), (ctx, right, part)]
    peers += [(lax.rem(ctx + i, groups), head, part) for i in range(1, groups)]
    active = lax.rem(ctx + groups - shift, 4) != 3
    return ctx, head, part, shift, right, left, peers, active


def front_kernel(
    groups, ring, heads, patch_ref, wq_ref, wk_ref, wv_ref, out_ref,
    rows_all, weights, stage, weight_sem, own_sem, left_sem, right_sem, pass_sem, far_sem,
    give_sem, self_sem, take_sem,
):
    tokens, width = patch_ref.shape
    chunk = FRONT_ROWS
    chunks = tokens // chunk
    ctx, head, part, shift, right, left, peers, active = whereabouts(groups, ring)
    across = lax.rem(head + 2, ring)

    loads = [
        pltpu.make_async_copy(ref, weights.at[i], weight_sem.at[i])
        for i, ref in enumerate((wq_ref, wk_ref, wv_ref))
    ]
    for load in loads:
        load.start()
    sync_peers(peers)

    def span(c):
        return pl.ds(pl.multiple_of(c * chunk, chunk), chunk)

    def own_copy(c, way, to, sems):
        return pltpu.make_async_remote_copy(
            src_ref=patch_ref.at[span(c), :],
            dst_ref=rows_all.at[head, span(c), :],
            send_sem=own_sem.at[way, c],
            recv_sem=sems.at[c],
            device_id=(ctx, to, part),
            device_id_type=MESH,
        )

    def arrival(slot, c, sems):
        return pltpu.make_async_copy(
            rows_all.at[slot, span(c), :], rows_all.at[slot, span(c), :], sems.at[c]
        )

    def send_own(c):
        own_copy(c, 0, right, left_sem).start()
        own_copy(c, 1, left, right_sem).start()

    def half(c, i):
        return pl.ds(pl.multiple_of(c * chunk + i * (chunk // 2), chunk // 2), chunk // 2)

    def pass_copy(c, i):
        slot, to = ((left, right), (right, left))[i]
        return pltpu.make_async_remote_copy(
            src_ref=rows_all.at[slot, half(c, i), :],
            dst_ref=rows_all.at[slot, half(c, i), :],
            send_sem=pass_sem.at[i, c],
            recv_sem=far_sem.at[i, c],
            device_id=(ctx, to, part),
            device_id_type=MESH,
        )

    def far_arrival(c, i):
        return pltpu.make_async_copy(
            rows_all.at[across, half(c, i), :], rows_all.at[across, half(c, i), :], far_sem.at[i, c]
        )

    def give_copy(c, i):
        target = lax.rem(ctx + i, groups)
        unit = lax.rem(target + groups - shift, groups)
        owner = jnp.minimum(unit - unit // 4, heads - 1)
        return lax.rem(unit, 4) != 3, pltpu.make_async_remote_copy(
            src_ref=stage.at[owner, span(c), :],
            dst_ref=out_ref.at[ctx, span(c), :],
            send_sem=give_sem.at[i - 1, c],
            recv_sem=take_sem,
            device_id=(target, head, part),
            device_id_type=MESH,
        )

    def keep_copy(c):
        unit = lax.rem(ctx + groups - shift, groups)
        owner = jnp.minimum(unit - unit // 4, heads - 1)
        return pltpu.make_async_copy(
            stage.at[owner, span(c), :], out_ref.at[ctx, span(c), :], self_sem.at[c]
        )

    def project_chunk(c):
        for pair in range(heads // 2):
            cols = slice(pair * 2 * HDIM, (pair + 1) * 2 * HDIM)
            for i in range(3):
                total = jnp.dot(
                    rows_all[0, span(c), :], weights[i, :width, cols],
                    preferred_element_type=jnp.float32,
                )
                for k in range(1, ring):
                    total += jnp.dot(
                        rows_all[k, span(c), :], weights[i, k * width : (k + 1) * width, cols],
                        preferred_element_type=jnp.float32,
                    )
                total = total.astype(jnp.bfloat16)
                for j in range(2):
                    stage[2 * pair + j, span(c), i * HDIM : (i + 1) * HDIM] = total[
                        :, j * HDIM : (j + 1) * HDIM
                    ]
        for i in FRONT_ORDER:
            owned, copy = give_copy(c, i)

            @pl.when(owned)
            def _():
                copy.start()

        @pl.when(active)
        def _():
            keep_copy(c).start()

    ahead = min(FRONT_AHEAD, chunks)
    for c in range(ahead):
        send_own(c)
    mine = pltpu.make_async_copy(patch_ref, rows_all.at[head], weight_sem.at[3])
    mine.start()

    def step(c, carry):
        @pl.when(c < chunks)
        def _():
            arrival(left, c, left_sem).wait()
            pass_copy(c, 0).start()
            arrival(right, c, right_sem).wait()
            pass_copy(c, 1).start()

        @pl.when(c + ahead < chunks)
        def _():
            send_own(c + ahead)

        @pl.when(c >= FRONT_LAG)
        def _():
            for i in range(2):
                far_arrival(c - FRONT_LAG, i).wait()

            @pl.when(c == FRONT_LAG)
            def _():
                mine.wait()
                for load in loads:
                    load.wait()

            project_chunk(c - FRONT_LAG)

        return carry

    lax.fori_loop(0, chunks + FRONT_LAG, step, 0)

    def settle(c, carry):
        own_copy(c, 0, right, left_sem).wait_send()
        own_copy(c, 1, left, right_sem).wait_send()
        pass_copy(c, 0).wait_send()
        pass_copy(c, 1).wait_send()
        for i in range(1, groups):
            owned, copy = give_copy(c, i)

            @pl.when(owned)
            def _():
                copy.wait_send()

        @pl.when(active)
        def _():
            keep_copy(c).wait()

        return carry

    lax.fori_loop(0, chunks, settle, 0)

    @pl.when(active)
    def _():
        others = pl.ds(0, groups - 1)
        pltpu.make_async_copy(out_ref.at[others], out_ref.at[others], take_sem).wait()


def front(groups, ring, patch_rows, query_weight, key_weight, value_weight):
    tokens, width = patch_rows.shape
    depth, columns = query_weight.shape
    heads = columns // HDIM
    chunks = tokens // FRONT_ROWS
    dma = pltpu.SemaphoreType.DMA
    return pl.pallas_call(
        functools.partial(front_kernel, groups, ring, heads),
        out_shape=jax.ShapeDtypeStruct((groups, tokens, 3 * HDIM), jnp.bfloat16),
        in_specs=[pl.BlockSpec(memory_space=pl.ANY)] * 4,
        out_specs=pl.BlockSpec(memory_space=pl.ANY),
        scratch_shapes=[
            pltpu.VMEM((ring, tokens, width), jnp.bfloat16),
            pltpu.VMEM((3, depth, columns), jnp.bfloat16),
            pltpu.VMEM((heads, tokens, 3 * HDIM), jnp.bfloat16),
            dma((4,)),
            dma((2, chunks)),
            dma((chunks,)),
            dma((chunks,)),
            dma((2, chunks)),
            dma((2, chunks)),
            dma((groups - 1, chunks)),
            dma((chunks,)),
            dma,
        ],
        compiler_params=pltpu.CompilerParams(
            collective_id=0, has_side_effects=True, vmem_limit_bytes=60 * 1024 * 1024
        ),
        cost_estimate=pl.CostEstimate(
            flops=6 * tokens * depth * columns, bytes_accessed=8 * depth * columns, transcendentals=0
        ),
        name="front",
    )(patch_rows, query_weight, key_weight, value_weight)


def back_kernel(
    groups, ring, heads, att_ref, wo_ref, out_ref,
    gathered, weights, far_out, far_in, side_out, side_in, own, pending,
    weight_sem, give_sem, self_sem, take_sem, far_send, far_recv, side_send, side_recv,
):
    tokens, width = out_ref.shape
    chunk = BACK_ROWS
    chunks = tokens // chunk
    ctx, head, part, shift, right, left, peers, active = whereabouts(groups, ring)
    across = lax.rem(head + 2, ring)
    unit = lax.rem(ctx + groups - shift, groups)
    mine = jnp.minimum(unit - unit // 4, heads - 1)

    loads = [
        pltpu.make_async_copy(
            wo_ref.at[:, pl.ds(pl.multiple_of(block * width, width), width)],
            weights.at[i],
            weight_sem.at[i],
        )
        for i, block in enumerate((across, right, left, head))
    ]
    for load in loads:
        load.start()
    sync_peers(peers)

    def span(c):
        return pl.ds(pl.multiple_of(c * chunk, chunk), chunk)

    def give_copy(c, i):
        source = lax.rem(ctx + i, groups)
        return pltpu.make_async_remote_copy(
            src_ref=att_ref.at[source, span(c), :],
            dst_ref=gathered.at[mine, span(c), :],
            send_sem=give_sem.at[i - 1, c],
            recv_sem=take_sem.at[c],
            device_id=(source, head, part),
            device_id_type=MESH,
        )

    def keep_copy(c):
        return pltpu.make_async_copy(
            att_ref.at[ctx, span(c), :], gathered.at[mine, span(c), :], self_sem.at[c]
        )

    @pl.when(active)
    def _():
        def give(c, carry):
            keep_copy(c).start()
            for i in range(1, groups):
                give_copy(c, i).start()
            return carry

        lax.fori_loop(0, chunks, give, 0)

    def half(c, i):
        return pl.ds(pl.multiple_of(c * chunk + i * (chunk // 2), chunk // 2), chunk // 2)

    def far_copy(c, i):
        return pltpu.make_async_remote_copy(
            src_ref=far_out.at[half(c, i), :],
            dst_ref=far_in.at[half(c, i), :],
            send_sem=far_send.at[i, c],
            recv_sem=far_recv.at[i, c],
            device_id=(ctx, (right, left)[i], part),
            device_id_type=MESH,
        )

    def side_copy(c, way, i):
        return pltpu.make_async_remote_copy(
            src_ref=side_out.at[way, half(c, i), :],
            dst_ref=side_in.at[way, half(c, i), :],
            send_sem=side_send.at[2 * way + i, c],
            recv_sem=side_recv.at[2 * way + i, c],
            device_id=(ctx, (right, left)[way], part),
            device_id_type=MESH,
        )

    for load in loads:
        load.wait()

    def mix(c):
        @pl.when(active)
        def _():
            keep_copy(c).wait()
            others = pl.ds(0, heads - 1)
            pltpu.make_async_copy(
                gathered.at[others, span(c), :], gathered.at[others, span(c), :], take_sem.at[c]
            ).wait()

        @pl.when(jnp.logical_not(active))
        def _():
            pltpu.make_async_copy(
                gathered.at[:, span(c), :], gathered.at[:, span(c), :], take_sem.at[c]
            ).wait()

        rows = jnp.concatenate([gathered[h, span(c), :] for h in range(heads)], axis=1)

        def part_sum(i):
            return jnp.dot(rows, weights[i], preferred_element_type=jnp.float32)

        far_out[span(c), :] = part_sum(0).astype(jnp.bfloat16)
        far_copy(c, 0).start()
        far_copy(c, 1).start()
        middle = chunk // 2
        to_right, to_left = part_sum(1), part_sum(2)
        side_out[0, half(c, 1), :] = to_right[middle:].astype(jnp.bfloat16)
        side_copy(c, 0, 1).start()
        side_out[1, half(c, 0), :] = to_left[:middle].astype(jnp.bfloat16)
        side_copy(c, 1, 0).start()
        pending[half(c, 0), :] = to_right[:middle]
        pending[half(c, 1), :] = to_left[middle:]
        own[span(c), :] = part_sum(3)

    def merge(c):
        for i in range(2):
            far_copy(c, i).wait_recv()
            side_out[i, half(c, i), :] = (
                pending[half(c, i), :] + far_in[half(c, i), :].astype(jnp.float32)
            ).astype(jnp.bfloat16)
            side_copy(c, i, i).start()

    def close(c):
        for way in range(2):
            for i in range(2):
                side_copy(c, way, i).wait_recv()
        out_ref[span(c), :] = (
            own[span(c), :]
            + side_in[0, span(c), :].astype(jnp.float32)
            + side_in[1, span(c), :].astype(jnp.float32)
        ).astype(jnp.bfloat16)

    def step(c, carry):
        @pl.when((c >= BACK_LAG) & (c < chunks + BACK_LAG))
        def _():
            merge(c - BACK_LAG)

        @pl.when(c < chunks)
        def _():
            mix(c)

        @pl.when(c >= 2 * BACK_LAG)
        def _():
            close(c - 2 * BACK_LAG)

        return carry

    lax.fori_loop(0, chunks + 2 * BACK_LAG, step, 0)

    def settle(c, carry):
        for i in range(2):
            far_copy(c, i).wait_send()
            side_copy(c, 0, i).wait_send()
            side_copy(c, 1, i).wait_send()

        @pl.when(active)
        def _():
            for i in range(1, groups):
                give_copy(c, i).wait_send()

        return carry

    lax.fori_loop(0, chunks, settle, 0)


def back(groups, ring, attended, output_weight):
    tokens = attended.shape[1]
    columns, depth = output_weight.shape
    width = depth // ring
    heads = columns // HDIM
    chunks = tokens // BACK_ROWS
    dma = pltpu.SemaphoreType.DMA
    return pl.pallas_call(
        functools.partial(back_kernel, groups, ring, heads),
        out_shape=jax.ShapeDtypeStruct((tokens, width), jnp.bfloat16),
        in_specs=[pl.BlockSpec(memory_space=pl.ANY)] * 2,
        out_specs=pl.BlockSpec(memory_space=pltpu.VMEM),
        scratch_shapes=[
            pltpu.VMEM((heads, tokens, HDIM), jnp.bfloat16),
            pltpu.VMEM((ring, columns, width), jnp.bfloat16),
            pltpu.VMEM((tokens, width), jnp.bfloat16),
            pltpu.VMEM((tokens, width), jnp.bfloat16),
            pltpu.VMEM((2, tokens, width), jnp.bfloat16),
            pltpu.VMEM((2, tokens, width), jnp.bfloat16),
            pltpu.VMEM((tokens, width), jnp.float32),
            pltpu.VMEM((tokens, width), jnp.float32),
            dma((ring,)),
            dma((groups - 1, chunks)),
            dma((chunks,)),
            dma((chunks,)),
            dma((2, chunks)),
            dma((2, chunks)),
            dma((4, chunks)),
            dma((4, chunks)),
        ],
        compiler_params=pltpu.CompilerParams(
            collective_id=1, has_side_effects=True, vmem_limit_bytes=60 * 1024 * 1024
        ),
        cost_estimate=pl.CostEstimate(
            flops=2 * tokens * depth * columns, bytes_accessed=2 * depth * columns, transcendentals=0
        ),
        name="back",
    )(attended, output_weight)


def body(patch_rows, query_weight, key_weight, value_weight, output_weight, tile_slot, tile_mask):
    groups = lax.axis_size("ctx")
    tokens = patch_rows.shape[0]
    ring = lax.axis_size("head")
    sent = front(groups, ring, patch_rows, query_weight, key_weight, value_weight)

    def is_active():
        return whereabouts(groups, ring)[-1]

    attended = attend(is_active, tile_slot, tile_mask, sent.reshape(groups * tokens, 3 * HDIM))
    return back(groups, ring, attended.reshape(groups, tokens, HDIM), output_weight)


def solution(mesh):
    in_specs = (
        P(("dp", "ctx"), "head"),
        P(None, "head"),
        P(None, "head"),
        P(None, "head"),
        P("head", None),
        P("dp"),
        P("dp", None),
    )
    out_specs = P(("dp", "ctx"), "head")
    return jax.shard_map(body, mesh=mesh, in_specs=in_specs, out_specs=out_specs, check_vma=False)
```
